256 devices in a mesh: grp: 4 (over y_hi, core), tile: 64 (over y_lo, x, z).
Axes of the slice: x: 4, y: 4 (y_hi: 2, y_lo: 2; y = y_hi * 2 + y_lo), z: 8, core: 2. Of those that a mesh axis runs over, the one named last changes fastest.
Arguments:
- query_tokens: bfloat16 [24576, 3072], P('tile', 'grp'), may hold values from -5 to 5
- key_tokens: bfloat16 [24576, 3072], P('tile', 'grp'), may hold values from -5 to 5
- value_tokens: bfloat16 [24576, 3072], P('tile', 'grp'), may hold values from -6 to 6
- w_out: bfloat16 [3072, 1536], P('grp'), may hold values from -1.75 to 1.75
- cotangent: bfloat16 [24576, 1536], P('tile', 'grp'), may hold values from -1.5 to 1.5
- neighbours: int32 [64, 5], P('tile'), may hold values from -1 to 63, as said below
- tile_tokens: int32 [64], replicated, may hold values from 1 to 384, as said below
Outputs:
- block_out: bfloat16 [24576, 1536], P('tile', 'grp')
- query_grad: bfloat16 [24576, 3072], P('tile', 'grp')
- key_grad: bfloat16 [24576, 3072], P('tile', 'grp')
- value_grad: bfloat16 [24576, 3072], P('tile', 'grp')
- weight_grad: bfloat16 [3072, 1536], P('grp')
The draws below stay inside these ranges and needn't reach their ends.
Inputs may be any that keep to these rules, and one draw needn't show every extreme that they name: `neighbours`: row r lists distinct tiles: first r itself, then tiles at most one tile away from r in time, height and width; unused slots come last and hold -1; some rows use all 5 slots. `tile_tokens`: the live tokens of a tile are its first ones; every tile outside the last time tile and the last height tile holds all 384.
All inputs are finite; a program needn't handle non-finite values.
Results may differ from the reference program's by a relative error of at most 0.0074.
Values may be sent and summed in bfloat16 or wider, within the bound.
A program may use at most 192 MiB of HBM per device.

```python
import math
import jax
import jax.numpy as jnp
import numpy as np
from jax import lax

HEADS = 24
HEAD_DIM = 128
DOUT = 1536
TILE = 384
NB = 5
NH = 4
TW = 1
TT = 16
TILES = 64
TOKENS = 24576
FEAT = 3072
N_TILE = 64


def tile_layout():
    index = jnp.arange(TILES, dtype=jnp.int32)
    return (index, index // (NH * TW), index // TW % NH, index % TW)


def draw_query_tokens(key, part):
    key = jax.random.fold_in(key, 31)
    field = jnp.clip(jax.random.normal(key, (TILES, TILE, FEAT), jnp.float32), -5.0, 5.0)
    return field.reshape(TOKENS, FEAT).astype(jnp.bfloat16)


def draw_key_tokens(key, part):
    key = jax.random.fold_in(key, 32)
    field = jnp.clip(jax.random.normal(key, (TILES, TILE, FEAT), jnp.float32), -5.0, 5.0)
    return field.reshape(TOKENS, FEAT).astype(jnp.bfloat16)


def draw_neighbours(key, part):
    key = jax.random.fold_in(key, 41)
    first, second, third = jax.random.split(key, 3)
    index, time_pos, height_pos, width_pos = tile_layout()
    shifts = np.array([(time_step, height_step, width_step) for time_step in (-1, 0, 1) for height_step in (-1, 0, 1) for width_step in (-1, 0, 1) if (time_step, height_step, width_step) != (0, 0, 0)], dtype=np.int32)
    near_time = time_pos[:, None] + shifts[None, :, 0]
    near_height = height_pos[:, None] + shifts[None, :, 1]
    near_width = width_pos[:, None] + shifts[None, :, 2]
    inside = (near_time >= 0) & (near_time < TT) & (near_height >= 0) & (near_height < NH) & (near_width >= 0) & (near_width < TW)
    near_id = (near_time * NH + near_height) * TW + near_width
    ranking = jax.random.randint(first, (TILES, 26), 0, 1 << 20) * 32 + jnp.arange(26, dtype=jnp.int32)[None, :]
    ranking = jnp.where(inside, ranking + (1 << 26), ranking)
    order = jnp.argsort(-ranking, axis=1)
    ranked = jnp.take_along_axis(near_id, order, axis=1)
    available = jnp.sum(inside.astype(jnp.int32), axis=1)
    wanted = jax.random.randint(second, (TILES,), 2, NB + 1)
    filled = jax.random.randint(third, (TILES,), 0, 2)
    wanted = jnp.where(filled == 1, NB, wanted)
    wanted = jnp.where(index == (NH + 1) * TW, NB, wanted)
    wanted = jnp.minimum(wanted, available + 1)
    slot_pos = jnp.arange(1, NB, dtype=jnp.int32)[None, :]
    others = jnp.where(slot_pos < wanted[:, None], ranked[:, :NB - 1], -1)
    return jnp.concatenate([index[:, None], others], axis=1).astype(jnp.int32)


def draw_tile_tokens(key, part):
    key = jax.random.fold_in(key, 51)
    index, time_pos, height_pos, width_pos = tile_layout()
    border = (time_pos == TT - 1) | (height_pos == NH - 1)
    drawn = jax.random.randint(key, (TILES,), 1, TILE + 1)
    return jnp.where(border, drawn, TILE).astype(jnp.int32)


def levels(own_key, dims, shards, low, largest):
    factor_of = 1.0
    for axis_at, parts in shards:
        draws = jax.random.uniform(jax.random.fold_in(jax.random.fold_in(own_key, 6), axis_at), (parts,), jnp.float32, low / len(shards), largest / len(shards))
        factor_of = factor_of * jnp.repeat(jnp.exp(draws), dims[axis_at] // parts).reshape((-1,) + (1,) * (len(dims) - 1 - axis_at))
    return factor_of


def scatter_about(stream_key, shape, width, limit, cuts=(), held_as=jnp.bfloat16):
    level = levels(stream_key, shape, cuts, -0.22, 0.18) if cuts else 1.0
    entries = jax.random.normal(stream_key, shape, jnp.float32) * width * level
    return jnp.minimum(jnp.maximum(entries, -limit), limit).astype(held_as)


def setup_inputs(seed: int = 0) -> dict:
    key_list = jax.random.split(jax.random.key(seed), 8)
    return {
        "query_tokens": draw_query_tokens(jax.random.fold_in(key_list[7], 71), 0),
        "key_tokens": draw_key_tokens(jax.random.fold_in(key_list[7], 71), 0),
        "value_tokens": scatter_about(key_list[2], (TOKENS, FEAT), 1.0, 6.0, ((0, 64), (1, 4))),
        "w_out": scatter_about(key_list[3], (FEAT, DOUT), (max(1, HEADS * HEAD_DIM // 256)) ** -0.5, 1.75, ((0, 4),)),
        "cotangent": scatter_about(key_list[4], (TOKENS, DOUT), 0.25, 1.5, ((0, 64), (1, 4))),
        "neighbours": draw_neighbours(jax.random.fold_in(key_list[7], 71), 0),
        "tile_tokens": draw_tile_tokens(jax.random.fold_in(key_list[7], 71), 0),
    }


def softmax_rows(scores, live_mask):
    masked = jnp.where(live_mask[None, :], scores, jnp.float32(-1e+30))
    row_max = lax.optimization_barrier(jnp.max(masked, axis=1, keepdims=True))
    exponent = jnp.exp(masked - row_max)
    return exponent / lax.optimization_barrier(jnp.sum(exponent, axis=1, keepdims=True))

def head_pass(query_rows, near_keys, near_values, grad_rows, live_mask, factor):
    scores = jnp.dot(query_rows, near_keys.T, preferred_element_type=jnp.float32) * factor
    probability = softmax_rows(scores, live_mask)
    weights = probability.astype(jnp.bfloat16)
    attended = jnp.dot(weights, near_values, preferred_element_type=jnp.float32).astype(jnp.bfloat16)
    grad_prob = jnp.dot(grad_rows, near_values.T, preferred_element_type=jnp.float32)
    row_delta = lax.optimization_barrier(jnp.sum(probability * grad_prob, axis=1, keepdims=True))
    dscore = (probability * (grad_prob - row_delta) * factor).astype(jnp.bfloat16)
    grad_query = jnp.dot(dscore, near_keys, preferred_element_type=jnp.float32)
    grad_keys = jnp.dot(dscore.T, query_rows, preferred_element_type=jnp.float32)
    grad_values = jnp.dot(weights.T, grad_rows, preferred_element_type=jnp.float32)
    return (attended, grad_query, grad_keys, grad_values)

def split_heads(matrix):
    return matrix.reshape(matrix.shape[0], HEADS, HEAD_DIM).transpose(1, 0, 2)

def merge_heads(stacked):
    return stacked.transpose(1, 0, 2).reshape(stacked.shape[1], HEADS * HEAD_DIM)

def tile_pass(query_tile, near_keys, near_values, grad_tile, live_mask):
    factor = 1.0 / math.sqrt(HEAD_DIM)

    def one_head(inputs):
        return head_pass(inputs[0], inputs[1], inputs[2], inputs[3], live_mask, factor)
    results = lax.map(one_head, (split_heads(query_tile), split_heads(near_keys), split_heads(near_values), split_heads(grad_tile)))
    return tuple((merge_heads(result) for result in results))

def reference(query_tokens, key_tokens, value_tokens, w_out, cotangent, neighbours, tile_tokens):
    grad_attn = jnp.dot(cotangent, w_out.T, preferred_element_type=jnp.float32).astype(jnp.bfloat16)
    query_tiles = query_tokens.reshape(TILES, TILE, FEAT)
    key_tiles = key_tokens.reshape(TILES, TILE, FEAT)
    value_tiles = value_tokens.reshape(TILES, TILE, FEAT)
    grad_tiles = grad_attn.reshape(TILES, TILE, FEAT)
    positions = jnp.arange(TILE, dtype=jnp.int32)
    slot_ids = jnp.arange(9 * TW, dtype=jnp.int32)
    slot_time = slot_ids // (3 * TW)
    slot_height = slot_ids // TW % 3
    slot_width = slot_ids % TW
    centre = (slot_time == 1) & (slot_height == 1)

    def device_step(carried, device_pos):
        key_acc, value_acc = carried
        time_here = device_pos // NH
        height_here = device_pos % NH

        def tile_step(buffers, width_pos):
            key_buffer, value_buffer = buffers
            tile_pos = device_pos * TW + width_pos
            list_ids = neighbours[tile_pos]
            safe_ids = jnp.maximum(list_ids, 0)
            near_time = safe_ids // (NH * TW)
            near_height = safe_ids // TW % NH
            near_width = safe_ids % TW
            slot_index = ((near_time - time_here + 1) * 3 + (near_height - height_here + 1)) * TW + near_width
            slot_index = jnp.where(list_ids >= 0, slot_index, 4 * TW).astype(jnp.int32)
            counts = tile_tokens[safe_ids]
            live_mask = ((list_ids >= 0)[:, None] & (positions[None, :] < counts[:, None])).reshape(NB * TILE)
            near_keys = key_tiles[safe_ids].reshape(NB * TILE, FEAT)
            near_values = value_tiles[safe_ids].reshape(NB * TILE, FEAT)
            attended, grad_query, grad_keys, grad_values = tile_pass(query_tiles[tile_pos], near_keys, near_values, grad_tiles[tile_pos], live_mask)
            key_buffer = key_buffer.at[slot_index].add(grad_keys.reshape(NB, TILE, FEAT))
            value_buffer = value_buffer.at[slot_index].add(grad_values.reshape(NB, TILE, FEAT))
            return ((key_buffer, value_buffer), (attended, grad_query.astype(jnp.bfloat16)))
        zero_buffer = jnp.zeros((9 * TW, TILE, FEAT), jnp.float32)
        (key_buffer, value_buffer), (attended, grad_query) = lax.scan(tile_step, (zero_buffer, zero_buffer), jnp.arange(TW, dtype=jnp.int32))
        near_time = time_here + slot_time - 1
        near_height = height_here + slot_height - 1
        inside = (near_time >= 0) & (near_time < TT) & (near_height >= 0) & (near_height < NH)
        target = jnp.where(inside, (near_time * NH + near_height) * TW + slot_width, TILES).astype(jnp.int32)
        key_sent = lax.optimization_barrier(key_buffer.astype(jnp.bfloat16)).astype(jnp.float32)
        value_sent = lax.optimization_barrier(value_buffer.astype(jnp.bfloat16)).astype(jnp.float32)
        key_acc = key_acc.at[target].add(jnp.where(centre[:, None, None], key_buffer, key_sent), mode='drop')
        value_acc = value_acc.at[target].add(jnp.where(centre[:, None, None], value_buffer, value_sent), mode='drop')
        return ((key_acc, value_acc), (attended, grad_query))
    full_zero = jnp.zeros((TILES, TILE, FEAT), jnp.float32)
    (key_acc, value_acc), (attended, grad_query) = lax.scan(device_step, (full_zero, full_zero), jnp.arange(N_TILE, dtype=jnp.int32))
    attended = attended.reshape(TOKENS, FEAT)
    block_out = jnp.dot(attended, w_out, preferred_element_type=jnp.float32).astype(jnp.bfloat16)
    weight_grad = jnp.dot(attended.T, cotangent, preferred_element_type=jnp.float32).astype(jnp.bfloat16)
    query_grad = grad_query.reshape(TOKENS, FEAT)
    key_grad = key_acc.reshape(TOKENS, FEAT).astype(jnp.bfloat16)
    value_grad = value_acc.reshape(TOKENS, FEAT).astype(jnp.bfloat16)
    return (block_out, query_grad, key_grad, value_grad, weight_grad)
```

```python
import functools
import math

import jax
import jax.numpy as jnp
from jax import lax
from jax.experimental import pallas as pl
from jax.experimental.pallas import tpu as pltpu
from jax.sharding import PartitionSpec as P

MESH = pl.DeviceIdType.MESH
HEAD_DIM = 128
TILE = 384
NB = 5
HEADS = 6
RING = 8
RINGS = 8
FEAT = HEADS * HEAD_DIM
GRP = 4
DBLK = 384
DOUT = GRP * DBLK
FACTOR = 1.0 / math.sqrt(HEAD_DIM)
BF16 = jnp.bfloat16
F32 = jnp.float32
VMEM_LIMIT = 56 * 1024 * 1024


def whereabouts():
    tile = lax.axis_index("tile")
    grp = lax.axis_index("grp")
    z = tile % RING
    ring = tile // RING
    core = grp % 2
    idle = 3 - 2 * core
    return tile, grp, z, ring, core, idle


def owns(z, idle):
    return z % 4 != idle


def head_at(z, idle):
    zz = z % 4
    return (z // 4) * 3 + zz - jnp.where(zz > idle, 1, 0)


def place_of(head, idle):
    hh = head % 3
    return (head // 3) * 4 + hh + jnp.where(hh >= idle, 1, 0)


def head_cols(head):
    return pl.ds(pl.multiple_of(head * HEAD_DIM, HEAD_DIM), HEAD_DIM)


def remote(src, dst, send_sem, recv_sem, **where):
    return pltpu.make_async_remote_copy(
        src_ref=src,
        dst_ref=dst,
        send_sem=send_sem,
        recv_sem=recv_sem,
        device_id=where,
        device_id_type=MESH,
    )


def signal(barrier, **where):
    pl.semaphore_signal(barrier, inc=1, device_id=where, device_id_type=MESH)


def greet_ring(barrier, tile, z, ring):
    @pl.loop(1, RING)
    def _(s):
        signal(barrier, tile=tile - z + (z + s) % RING)

    @pl.when(ring > 0)
    def _():
        signal(barrier, tile=tile - RING)

    @pl.when(ring < RINGS - 1)
    def _():
        signal(barrier, tile=tile + RING)


def ring_edges(ring):
    return jnp.where(ring > 0, 1, 0) + jnp.where(ring < RINGS - 1, 1, 0)


def inbound_kernel(
    nb, q, k, v, cot, w,
    nb8, q8, k16, v16, g8, cotf,
    cot_s, g_loc, ssem, rsem, lsem, csend, crecv, clocal, hsend, hrecv,
):
    tile, grp, z, ring, core, idle = whereabouts()
    base = tile - z
    mine = owns(z, idle)
    barrier = pltpu.get_barrier_semaphore()
    greet_ring(barrier, tile, z, ring)
    other_core = grp + 1 - 2 * core
    other_y = (grp + 2) % GRP
    signal(barrier, grp=other_core)
    signal(barrier, grp=other_y)
    pl.semaphore_wait(barrier, RING - 1 + 2 + ring_edges(ring))

    to_y = remote(cot, cot_s.at[grp], csend.at[0], crecv.at[0], grp=other_y)
    to_core = remote(cot, cot_s.at[grp], csend.at[1], crecv.at[1], grp=other_core)
    to_y.start()
    to_core.start()
    keep = pltpu.make_async_copy(cot, cot_s.at[grp], clocal.at[0])
    keep.start()

    def ends(kind, at):
        cols = head_cols(head_at(at, idle))
        if kind == 0:
            return k.at[:, cols], k16.at[z + 4]
        if kind == 1:
            return v.at[:, cols], v16.at[z + 4]
        if kind == 2:
            return q.at[:, cols], q8.at[z]
        if kind == 3:
            return g_loc.at[head_at(at, idle)], g8.at[z]
        return nb.at[0], nb8.at[z]

    def send(kind, s):
        at = (z + s) % RING
        src, dst = ends(kind, at)
        return remote(src, dst, ssem.at[kind, s], rsem.at[kind, z], tile=base + at)

    def keep_own(kind):
        src, dst = ends(kind, z)
        return pltpu.make_async_copy(src, dst, lsem.at[kind])

    def arrived(kind, at):
        dst = (k16.at[at + 4], v16.at[at + 4], q8.at[at], g8.at[at], nb8.at[at])[kind]
        return remote(dst, dst, ssem.at[kind, 0], rsem.at[kind, at], tile=base + at)

    for kinds in ((0, 1), (2, 4)):
        @pl.loop(1, RING)
        def _(s):
            @pl.when(owns(z + s, idle))
            def _():
                for kind in kinds:
                    send(kind, s).start()

    @pl.when(mine)
    def _():
        for kind in (0, 1, 2, 4):
            keep_own(kind).start()

    remote(cot, cot_s.at[other_y], csend.at[0], crecv.at[0], grp=other_y).wait_recv()
    on = remote(cot_s.at[other_y], cot_s.at[other_y], csend.at[2], crecv.at[2], grp=other_core)
    on.start()
    far = (other_core + 2) % GRP
    remote(cot, cot_s.at[other_core], csend.at[1], crecv.at[1], grp=other_core).wait_recv()
    remote(cot, cot_s.at[far], csend.at[2], crecv.at[2], grp=other_core).wait_recv()
    keep.wait()
    out = pltpu.make_async_copy(cot_s, cotf, clocal.at[1])
    out.start()

    @pl.loop(0, RING)
    def _(s):
        at = (z + s) % RING

        @pl.when(owns(at, idle))
        def _():
            head = head_at(at, idle)
            rows = head_cols(head)
            total = None
            for b in range(GRP):
                part = lax.dot_general(
                    cot_s[b], w[rows, b * DBLK:(b + 1) * DBLK],
                    (((1,), (1,)), ((), ())), preferred_element_type=F32,
                )
                total = part if total is None else total + part
            g_loc[head] = total.astype(BF16)

            @pl.when(s > 0)
            def _():
                send(3, s).start()

            @pl.when(s == 0)
            def _():
                keep_own(3).start()

    def hop(kind, at, start):
        buf = (k16, v16)[kind]

        @pl.when((at >= 4) & (ring < RINGS - 1))
        def _():
            c = remote(buf.at[at + 4], buf.at[at - 4], hsend.at[kind, at], hrecv.at[kind, at],
                       tile=tile + RING)
            if start:
                c.start()
            else:
                c.wait_send()

        @pl.when((at < 4) & (ring > 0))
        def _():
            c = remote(buf.at[at + 4], buf.at[at + 12], hsend.at[kind, at], hrecv.at[kind, at],
                       tile=tile - RING)
            if start:
                c.start()
            else:
                c.wait_send()

    def hop_arrived(kind, at):
        buf = (k16, v16)[kind]

        @pl.when((at >= 4) & (ring > 0))
        def _():
            remote(buf.at[at - 4], buf.at[at - 4], hsend.at[kind, at], hrecv.at[kind, at],
                   tile=tile - RING).wait_recv()

        @pl.when((at < 4) & (ring < RINGS - 1))
        def _():
            remote(buf.at[at + 12], buf.at[at + 12], hsend.at[kind, at], hrecv.at[kind, at],
                   tile=tile + RING).wait_recv()

    @pl.when(mine)
    def _():
        for kind in (0, 1):
            keep_own(kind).wait()
            hop(kind, z, True)

        @pl.loop(1, RING)
        def _(s):
            at = (z + RING - s) % RING
            for kind in (0, 1):
                arrived(kind, at).wait_recv()
                hop(kind, at, True)

        for kind in (2, 3, 4):
            keep_own(kind).wait()

        @pl.loop(1, RING)
        def _(s):
            at = (z + RING - s) % RING
            for kind in (2, 3, 4):
                arrived(kind, at).wait_recv()

        @pl.loop(0, RING)
        def _(at):
            for kind in (0, 1):
                hop_arrived(kind, at)
                hop(kind, at, False)

    @pl.loop(1, RING)
    def _(s):
        @pl.when(owns(z + s, idle))
        def _():
            for kind in range(5):
                send(kind, s).wait_send()

    to_y.wait_send()
    to_core.wait_send()
    on.wait_send()
    out.wait()


def inbound(nb, q, k, v, cot, w):
    any_space = pl.BlockSpec(memory_space=pl.ANY)
    vmem = pl.BlockSpec(memory_space=pltpu.VMEM)
    dma = pltpu.SemaphoreType.DMA
    return pl.pallas_call(
        inbound_kernel,
        out_shape=(
            jax.ShapeDtypeStruct((RING, 8, 128), jnp.int32),
            jax.ShapeDtypeStruct((RING, TILE, HEAD_DIM), BF16),
            jax.ShapeDtypeStruct((2 * RING, TILE, HEAD_DIM), BF16),
            jax.ShapeDtypeStruct((2 * RING, TILE, HEAD_DIM), BF16),
            jax.ShapeDtypeStruct((RING, TILE, HEAD_DIM), BF16),
            jax.ShapeDtypeStruct((GRP, TILE, DBLK), BF16),
        ),
        in_specs=[any_space, any_space, any_space, any_space, vmem, vmem],
        out_specs=(any_space,) * 6,
        scratch_shapes=[
            pltpu.VMEM((GRP, TILE, DBLK), BF16),
            pltpu.VMEM((HEADS, TILE, HEAD_DIM), BF16),
            dma((5, RING)),
            dma((5, RING)),
            dma((5,)),
            dma((3,)),
            dma((3,)),
            dma((2,)),
            dma((2, RING)),
            dma((2, RING)),
        ],
        compiler_params=pltpu.CompilerParams(
            collective_id=0, has_side_effects=True, vmem_limit_bytes=VMEM_LIMIT
        ),
        name="inbound",
    )(nb, q, k, v, cot, w)


def attention_kernel(
    nb, tokens, q_ref, g_ref, k_ref, v_ref,
    att_ref, dq_ref, dko, dvo, dkh, dvh,
    acck, accv, e_scr,
):
    tile, grp, z, ring, core, idle = whereabouts()
    r = pl.program_id(0)

    @pl.when(owns(z, idle))
    def _():
        @pl.when(r == 0)
        def _():
            acck[...] = jnp.zeros_like(acck)
            accv[...] = jnp.zeros_like(accv)

        live = jnp.int32(0)
        for j in range(NB):
            live += jnp.where(nb[r, 0, j] >= 0, 1, 0)
        q = q_ref[0]
        g = g_ref[0]
        rows = lax.broadcasted_iota(jnp.int32, (TILE, TILE), 0)

        def local(j):
            return nb[r, 0, j] - ring * RING + 4

        def scores(j, top):
            s = lax.dot_general(
                k_ref[local(j)], q, (((1,), (1,)), ((), ())), preferred_element_type=F32
            )
            s = jnp.where(rows < tokens[nb[r, 0, j]], s, F32(-1e30))
            e_scr[j] = s
            return jnp.maximum(top, jnp.max(s, axis=0, keepdims=True))

        top = lax.fori_loop(0, live, scores, jnp.full((1, TILE), -1e30, F32))

        def exponents(j, total):
            e = jnp.exp2((e_scr[j] - top) * F32(FACTOR * math.log2(math.e)))
            e_scr[j] = e
            return total + jnp.sum(e, axis=0, keepdims=True)

        total = lax.fori_loop(0, live, exponents, jnp.zeros((1, TILE), F32))
        inverse = 1.0 / total

        def forward(j, out):
            p = e_scr[j] * inverse
            e_scr[j] = p
            return out + lax.dot_general(
                v_ref[local(j)], p.astype(BF16), (((0,), (0,)), ((), ())),
                preferred_element_type=F32,
            )

        out = lax.fori_loop(0, live, forward, jnp.zeros((HEAD_DIM, TILE), F32))
        att_ref[0] = out.T.astype(BF16)
        delta = jnp.sum(out * g.astype(F32).T, axis=0, keepdims=True)

        def backward(j, dq):
            at = local(j)
            p = e_scr[j]
            kk = k_ref[at]
            gp = lax.dot_general(
                v_ref[at], g, (((1,), (1,)), ((), ())), preferred_element_type=F32
            )
            ds = (p * (gp - delta) * F32(FACTOR)).astype(BF16)
            accv[at] += jnp.dot(p.astype(BF16), g, preferred_element_type=F32)
            acck[at] += jnp.dot(ds, q, preferred_element_type=F32)
            return dq + lax.dot_general(
                kk, ds, (((0,), (0,)), ((), ())), preferred_element_type=F32
            )

        dq = lax.fori_loop(0, live, backward, jnp.zeros((HEAD_DIM, TILE), F32))
        dq_ref[0] = dq.T.astype(BF16)

        @pl.when(r == RING - 1)
        def _():
            dko[...] = acck[4:12]
            dvo[...] = accv[4:12]
            dkh[0:4] = acck[0:4].astype(BF16)
            dkh[4:8] = acck[12:16].astype(BF16)
            dvh[0:4] = accv[0:4].astype(BF16)
            dvh[4:8] = accv[12:16].astype(BF16)


def attention(nb8, tokens, q8, g8, k16, v16):
    smem = pl.BlockSpec(memory_space=pltpu.SMEM)
    one = pl.BlockSpec((1, TILE, HEAD_DIM), lambda i: (i, 0, 0))

    def whole(n):
        return pl.BlockSpec((n, TILE, HEAD_DIM), lambda i: (0, 0, 0))

    def shape(n, dtype):
        return jax.ShapeDtypeStruct((n, TILE, HEAD_DIM), dtype)

    return pl.pallas_call(
        attention_kernel,
        grid=(RING,),
        out_shape=(
            shape(RING, BF16), shape(RING, BF16), shape(RING, F32), shape(RING, F32),
            shape(RING, BF16), shape(RING, BF16),
        ),
        in_specs=[smem, smem, one, one, whole(2 * RING), whole(2 * RING)],
        out_specs=(one, one, whole(RING), whole(RING), whole(RING), whole(RING)),
        scratch_shapes=[
            pltpu.VMEM((2 * RING, TILE, HEAD_DIM), F32),
            pltpu.VMEM((2 * RING, TILE, HEAD_DIM), F32),
            pltpu.VMEM((NB, TILE, TILE), F32),
        ],
        compiler_params=pltpu.CompilerParams(vmem_limit_bytes=VMEM_LIMIT),
        name="attention",
    )(nb8, tokens, q8, g8, k16, v16)


XROWS = FEAT // 4
YROWS = XROWS // 2
ZROWS = YROWS // 2
ZCOLS = DOUT // 4
HALF = DOUT // 2


def outbound_kernel(
    att8, dq8, dko, dvo, dkh, dvh, cot_s, w,
    bo, dq, dk, dv, dw,
    att_s, hk, hv, dkb, dvb, dwp, xl, xs, xacc, ys, yl, zs, zl, fin, pos, pol, own, ybs, ybl,
    ssem, rsem, lsem, hsend, hrecv, xsend, xrecv, ysend, yrecv, zsend, zrecv, gsend, grecv,
):
    tile, grp, z, ring, core, idle = whereabouts()
    base = tile - z
    mine = owns(z, idle)
    head = head_at(z, idle)
    x = ring % 4
    y = ring // 4
    right = tile - x * RING + (x + 1) % 4 * RING
    left = tile - x * RING + (x + 3) % 4 * RING
    y_pair = tile + 32 - 64 * y
    other_core = grp + 1 - 2 * core
    other_y = (grp + 2) % GRP
    y_hi = grp // 2

    barrier = pltpu.get_barrier_semaphore()
    greet_ring(barrier, tile, z, ring)
    signal(barrier, tile=right)
    signal(barrier, tile=left)
    signal(barrier, tile=y_pair)
    signal(barrier, grp=other_core)
    signal(barrier, grp=other_y)
    pl.semaphore_wait(barrier, RING - 1 + 5 + ring_edges(ring))

    def ends(kind, at, h):
        src = (att8, dq8, dkb, dvb)[kind].at[at]
        dst = (att_s, dq, dk, dv)[kind].at[:, head_cols(h)]
        return src, dst

    def send(kind, s):
        at = (z + s) % RING
        src, dst = ends(kind, at, head)
        return remote(src, dst, ssem.at[kind, s], rsem.at[kind, head], tile=base + at)

    def keep_own(kind):
        src, dst = ends(kind, z, head)
        return pltpu.make_async_copy(src, dst, lsem.at[kind])

    def start_all(kind):
        keep_own(kind).start()

        @pl.loop(1, RING)
        def _(s):
            send(kind, s).start()

    def wait_all(kind):
        @pl.loop(0, HEADS)
        def _(h):
            at = place_of(h, idle)
            src, dst = ends(kind, z, h)

            @pl.when(at != z)
            def _():
                remote(src, dst, ssem.at[kind, 0], rsem.at[kind, h], tile=base + at).wait_recv()

        @pl.when(mine)
        def _():
            keep_own(kind).wait()

    def sent_all(kind):
        @pl.loop(1, RING)
        def _(s):
            send(kind, s).wait_send()

    def halo(kind, up):
        src, dst = ((dkh, hk), (dvh, hv))[kind]
        if up:
            return remote(src.at[pl.ds(4, 4)], dst.at[pl.ds(0, 4)], hsend.at[kind, 1],
                          hrecv.at[kind, 0], tile=tile + RING)
        return remote(src.at[pl.ds(0, 4)], dst.at[pl.ds(4, 4)], hsend.at[kind, 0],
                      hrecv.at[kind, 1], tile=tile - RING)

    @pl.when(mine)
    def _():
        start_all(0)
        for kind in (0, 1):
            @pl.when(ring > 0)
            def _():
                halo(kind, False).start()

            @pl.when(ring < RINGS - 1)
            def _():
                halo(kind, True).start()

        start_all(1)

    wait_all(0)

    @pl.loop(0, HEADS)
    def _(h):
        rows = head_cols(h)
        turned = att_s[:, rows].T
        for b in range(GRP):
            dwp[rows, b * DBLK:(b + 1) * DBLK] = jnp.dot(
                turned, cot_s[b], preferred_element_type=F32
            ).astype(BF16)

    def xblock(i):
        return pl.ds(pl.multiple_of(i % 4 * XROWS, XROWS), XROWS)

    half_a, half_b = pl.ds(0, HALF), pl.ds(HALF, HALF)
    rel_a = remote(dwp.at[xblock(x + 2), half_a], xl.at[0], xsend.at[0], xrecv.at[0], tile=left)
    rel_b = remote(dwp.at[xblock(x + 2), half_b], xl.at[1], xsend.at[1], xrecv.at[1], tile=right)
    one_a = remote(dwp.at[xblock(x + 1), half_a], xl.at[2], xsend.at[2], xrecv.at[2], tile=right)
    one_b = remote(dwp.at[xblock(x + 3), half_b], xl.at[3], xsend.at[3], xrecv.at[3], tile=left)
    sum_a = remote(xs.at[0], xl.at[4], xsend.at[4], xrecv.at[4], tile=left)
    sum_b = remote(xs.at[1], xl.at[5], xsend.at[5], xrecv.at[5], tile=right)
    for c in (rel_a, rel_b, one_a, one_b):
        c.start()

    def projected(b):
        cols = pl.ds(pl.multiple_of(b * DBLK, DBLK), DBLK)
        return jnp.dot(att_s[...], w[:, cols], preferred_element_type=F32)

    @pl.loop(0, 2)
    def _(yy):
        pos[yy] = projected(yy * 2 + 1 - core)

    to_core = remote(pos, pol, gsend.at[0], grecv.at[0], grp=other_core)
    to_core.start()

    @pl.loop(0, 2)
    def _(yy):
        own[yy] = projected(yy * 2 + core)

    rel_a.wait_recv()
    xs[0] = (xl[0].astype(F32) + dwp[xblock(x + 3), half_a].astype(F32)).astype(BF16)
    sum_a.start()
    rel_b.wait_recv()
    xs[1] = (xl[1].astype(F32) + dwp[xblock(x + 1), half_b].astype(F32)).astype(BF16)
    sum_b.start()

    to_core.wait_recv()
    ybs[...] = (own[1 - y_hi] + pol[1 - y_hi]).astype(BF16)
    to_y = remote(ybs, ybl, gsend.at[1], grecv.at[1], grp=other_y)
    to_y.start()

    @pl.when(mine)
    def _():
        for kind in (0, 1):
            full, got, out = ((dko, hk, dkb), (dvo, hv, dvb))[kind]

            def back(up, first, has):
                @pl.when(has)
                def _():
                    halo(kind, up).wait_recv()

                    @pl.loop(first, first + 4)
                    def _(i):
                        out[i] = (full[i] + got[i].astype(F32)).astype(BF16)

                @pl.when(jnp.logical_not(has))
                def _():
                    @pl.loop(first, first + 4)
                    def _(i):
                        out[i] = full[i].astype(BF16)

            back(True, 0, ring > 0)
            back(False, 4, ring < RINGS - 1)
            start_all(2 + kind)

    one_a.wait_recv()
    sum_a.wait_recv()
    xacc[:, :HALF] = (
        dwp[xblock(x), :HALF].astype(F32) + xl[2].astype(F32) + xl[4].astype(F32)
    )
    one_b.wait_recv()
    sum_b.wait_recv()
    xacc[:, HALF:] = (
        dwp[xblock(x), HALF:].astype(F32) + xl[3].astype(F32) + xl[5].astype(F32)
    )
    my_rows = pl.ds(pl.multiple_of(y * YROWS, YROWS), YROWS)
    ys[...] = xacc[pl.ds(pl.multiple_of((1 - y) * YROWS, YROWS), YROWS), :].astype(BF16)
    y_sum = remote(ys, yl, ysend.at[0], yrecv.at[0], tile=y_pair)
    y_sum.start()
    y_sum.wait_recv()
    zs[...] = (xacc[my_rows, :] + yl[...].astype(F32)).astype(BF16)

    def zpart(at):
        return (
            pl.ds(pl.multiple_of(at // 4 * ZROWS, ZROWS), ZROWS),
            pl.ds(pl.multiple_of(at % 4 * ZCOLS, ZCOLS), ZCOLS),
        )

    def z_sum(s):
        at = (z + s) % RING
        return remote(zs.at[zpart(at)], zl.at[z], zsend.at[0, s], zrecv.at[0, z], tile=base + at)

    @pl.loop(1, RING)
    def _(s):
        z_sum(s).start()

    to_y.wait_recv()
    bo[...] = (own[y_hi] + pol[y_hi] + ybl[...].astype(F32)).astype(BF16)

    def z_sum_got(at):
        return remote(zl.at[at], zl.at[at], zsend.at[0, 0], zrecv.at[0, at], tile=base + at)

    rows, cols = zpart(z)
    total = zs[rows, cols].astype(F32)
    for s in range(1, RING):
        at = (z + s) % RING
        z_sum_got(at).wait_recv()
        total += zl[at].astype(F32)
    fin[...] = total.astype(BF16)

    slab = x * XROWS + y * YROWS

    def home(at):
        rows = pl.ds(pl.multiple_of(slab + at // 4 * ZROWS, ZROWS), ZROWS)
        return dw.at[rows, zpart(at)[1]]

    def z_all(s):
        at = (z + s) % RING
        return remote(fin, home(z), zsend.at[1, s], zrecv.at[1, z], tile=base + at)

    @pl.loop(1, RING)
    def _(s):
        z_all(s).start()

    kept = pltpu.make_async_copy(fin, home(z), lsem.at[4])
    kept.start()
    kept.wait()

    @pl.loop(1, RING)
    def _(s):
        at = (z + s) % RING
        remote(fin, home(at), zsend.at[1, 0], zrecv.at[1, at], tile=base + at).wait_recv()

    def yslab(yy):
        return dw.at[pl.ds(pl.multiple_of(x * XROWS + yy * YROWS, YROWS), YROWS), :]

    y_all = remote(yslab(y), yslab(y), ysend.at[1], yrecv.at[1], tile=y_pair)
    y_all.start()
    remote(yslab(1 - y), yslab(1 - y), ysend.at[1], yrecv.at[1], tile=y_pair).wait_recv()

    def xslab(i, part):
        return dw.at[xblock(i), (half_a, half_b)[part]]

    def x_all(i, part, slot, to):
        return remote(xslab(i, part), xslab(i, part), xsend.at[slot], xrecv.at[slot], tile=to)

    outs = [
        x_all(x, 0, 6, right), x_all(x, 1, 7, left), x_all(x, 1, 8, right), x_all(x, 0, 9, left)
    ]
    for c in outs:
        c.start()
    x_all(x + 3, 0, 6, left).wait_recv()
    pass_a = x_all(x + 3, 0, 10, right)
    pass_a.start()
    x_all(x + 1, 1, 7, right).wait_recv()
    pass_b = x_all(x + 1, 1, 11, left)
    pass_b.start()
    x_all(x + 3, 1, 8, left).wait_recv()
    x_all(x + 1, 0, 9, right).wait_recv()
    x_all(x + 2, 0, 10, left).wait_recv()
    x_all(x + 2, 1, 11, right).wait_recv()

    for kind in (1, 2, 3):
        wait_all(kind)

    @pl.when(mine)
    def _():
        for kind in range(4):
            sent_all(kind)
        for kind in (0, 1):
            @pl.when(ring > 0)
            def _():
                halo(kind, False).wait_send()

            @pl.when(ring < RINGS - 1)
            def _():
                halo(kind, True).wait_send()

    for c in (rel_a, rel_b, one_a, one_b, sum_a, sum_b, to_core, to_y, y_sum, y_all, pass_a, pass_b):
        c.wait_send()
    for c in outs:
        c.wait_send()

    @pl.loop(1, RING)
    def _(s):
        z_sum(s).wait_send()
        z_all(s).wait_send()


def outbound(att8, dq8, dko, dvo, dkh, dvh, cotf, w):
    any_space = pl.BlockSpec(memory_space=pl.ANY)
    vmem = pl.BlockSpec(memory_space=pltpu.VMEM)
    dma = pltpu.SemaphoreType.DMA
    grad = jax.ShapeDtypeStruct((TILE, FEAT), BF16)
    return pl.pallas_call(
        outbound_kernel,
        out_shape=(
            jax.ShapeDtypeStruct((TILE, DBLK), BF16), grad, grad, grad,
            jax.ShapeDtypeStruct((FEAT, DOUT), BF16),
        ),
        in_specs=[any_space, any_space, vmem, vmem, any_space, any_space, vmem, vmem],
        out_specs=(vmem, any_space, any_space, any_space, any_space),
        scratch_shapes=[
            pltpu.VMEM((TILE, FEAT), BF16),
            pltpu.VMEM((RING, TILE, HEAD_DIM), BF16),
            pltpu.VMEM((RING, TILE, HEAD_DIM), BF16),
            pltpu.VMEM((RING, TILE, HEAD_DIM), BF16),
            pltpu.VMEM((RING, TILE, HEAD_DIM), BF16),
            pltpu.VMEM((FEAT, DOUT), BF16),
            pltpu.VMEM((6, XROWS, HALF), BF16),
            pltpu.VMEM((2, XROWS, HALF), BF16),
            pltpu.VMEM((XROWS, DOUT), F32),
            pltpu.VMEM((YROWS, DOUT), BF16),
            pltpu.VMEM((YROWS, DOUT), BF16),
            pltpu.VMEM((YROWS, DOUT), BF16),
            pltpu.VMEM((RING, ZROWS, ZCOLS), BF16),
            pltpu.VMEM((ZROWS, ZCOLS), BF16),
            pltpu.VMEM((2, TILE, DBLK), F32),
            pltpu.VMEM((2, TILE, DBLK), F32),
            pltpu.VMEM((2, TILE, DBLK), F32),
            pltpu.VMEM((TILE, DBLK), BF16),
            pltpu.VMEM((TILE, DBLK), BF16),
            dma((4, RING)),
            dma((4, HEADS)),
            dma((5,)),
            dma((2, 2)),
            dma((2, 2)),
            dma((12,)),
            dma((12,)),
            dma((2,)),
            dma((2,)),
            dma((2, RING)),
            dma((2, RING)),
            dma((2,)),
            dma((2,)),
        ],
        compiler_params=pltpu.CompilerParams(
            collective_id=1, has_side_effects=True, vmem_limit_bytes=VMEM_LIMIT
        ),
        name="outbound",
    )(att8, dq8, dko, dvo, dkh, dvh, cotf, w)


def body(query_tokens, key_tokens, value_tokens, w_out, cotangent, neighbours, tile_tokens):
    nb = jnp.pad(neighbours.reshape(1, 1, NB), ((0, 0), (0, 7), (0, 128 - NB)), constant_values=-1)
    nb8, q8, k16, v16, g8, cotf = inbound(
        nb, query_tokens, key_tokens, value_tokens, cotangent, w_out
    )
    att8, dq8, dko, dvo, dkh, dvh = attention(nb8, tile_tokens, q8, g8, k16, v16)
    return outbound(att8, dq8, dko, dvo, dkh, dvh, cotf, w_out)


def solution(mesh):
    placed = (
        P("tile", "grp"),
        P("tile", "grp"),
        P("tile", "grp"),
        P("grp", None),
        P("tile", "grp"),
        P("tile", None),
        P(),
    )
    return jax.shard_map(
        body,
        mesh=mesh,
        in_specs=placed,
        out_specs=(
            P("tile", "grp"),
            P("tile", "grp"),
            P("tile", "grp"),
            P("tile", "grp"),
            P("grp", None),
        ),
        check_vma=False,
    )
```

```python
import math

import jax
import jax.numpy as jnp
from jax import lax
from jax.experimental import pallas as pl
from jax.experimental.pallas import tpu as pltpu
from jax.sharding import PartitionSpec as P

MESH = pl.DeviceIdType.MESH
HEAD_DIM = 128
TILE = 384
NB = 5
HEADS = 6
RING = 8
RINGS = 8
FEAT = HEADS * HEAD_DIM
GRP = 4
DBLK = 384
DOUT = GRP * DBLK
FACTOR = 1.0 / math.sqrt(HEAD_DIM)
BF16 = jnp.bfloat16
F32 = jnp.float32
VMEM_LIMIT = 56 * 1024 * 1024


def whereabouts():
    tile = lax.axis_index("tile")
    grp = lax.axis_index("grp")
    z = tile % RING
    ring = tile // RING
    core = grp % 2
    idle = 3 - 2 * core
    return tile, grp, z, ring, core, idle


def owns(z, idle):
    return z % 4 != idle


def head_at(z, idle):
    zz = z % 4
    return (z // 4) * 3 + zz - jnp.where(zz > idle, 1, 0)


def place_of(head, idle):
    hh = head % 3
    return (head // 3) * 4 + hh + jnp.where(hh >= idle, 1, 0)


def head_cols(head):
    return pl.ds(pl.multiple_of(head * HEAD_DIM, HEAD_DIM), HEAD_DIM)


def remote(src, dst, send_sem, recv_sem, **where):
    return pltpu.make_async_remote_copy(
        src_ref=src,
        dst_ref=dst,
        send_sem=send_sem,
        recv_sem=recv_sem,
        device_id=where,
        device_id_type=MESH,
    )


def signal(barrier, **where):
    pl.semaphore_signal(barrier, inc=1, device_id=where, device_id_type=MESH)


def greet_ring(barrier, tile, z, ring):
    @pl.loop(1, RING)
    def _(s):
        signal(barrier, tile=tile - z + (z + s) % RING)

    @pl.when(ring > 0)
    def _():
        signal(barrier, tile=tile - RING)

    @pl.when(ring < RINGS - 1)
    def _():
        signal(barrier, tile=tile + RING)


def ring_edges(ring):
    return jnp.where(ring > 0, 1, 0) + jnp.where(ring < RINGS - 1, 1, 0)

XROWS = FEAT // 4
YROWS = FEAT // 2
SROWS = FEAT // 8
ZROWS = SROWS // 2
ZCOLS = DOUT // 4
HALF = DOUT // 2
QUARTER = DOUT // 4
KEYS = NB * TILE
SHIFTS = tuple((dt, dh) for dt in (-1, 0, 1) for dh in (-1, 0, 1) if (dt, dh) != (0, 0))
LOG2E = math.log2(math.e)


def nt(a, b):
    return lax.dot_general(a, b, (((1,), (1,)), ((), ())), preferred_element_type=F32)


def tn(a, b):
    return lax.dot_general(a, b, (((0,), (0,)), ((), ())), preferred_element_type=F32)


def step_kernel(
    listed, tokens, q, k, v, cot, w,
    bo, dq, dk, dv, dw,
    nb_o, nb_v, nb_s, k16, v16, q8, g8, cot_s, g_loc, s_scr, p, vc, kc, ds_s, tmp, o_t, acck, accv,
    att8, dq8, att_s, hk, hv, hks, hvs, dkb, dvb,
    dwp, x1, x2, xs1, xs2, x_tot, y1s, y1l, y2l, y2, zs, zl, fin, pos, pol, own, ybs, ybl,
    ssem, rsem, lsem, csend, crecv, clocal, khsend, khrecv, osend, orecv, olocal, hsend, hrecv,
    xsend, xrecv, ysend, yrecv, zsend, zrecv, gsend, grecv,
):
    tile, grp, z, ring, core, idle = whereabouts()
    base = tile - z
    mine = owns(z, idle)
    my_head = head_at(z, idle)
    x = ring % 4
    y = ring // 4
    right = tile - x * RING + (x + 1) % 4 * RING
    left = tile - x * RING + (x + 3) % 4 * RING
    y_pair = tile + 32 - 64 * y
    other_core = grp + 1 - 2 * core
    other_y = (grp + 2) % GRP
    y_hi = grp // 2
    has_up = ring < RINGS - 1
    has_down = ring > 0

    barrier = pltpu.get_barrier_semaphore()
    greet_ring(barrier, tile, z, ring)
    for where in (right, left, y_pair):
        signal(barrier, tile=where)
    signal(barrier, grp=other_core)
    signal(barrier, grp=other_y)
    pl.semaphore_wait(barrier, RING - 1 + 5 + ring_edges(ring))

    cot_y = remote(cot, cot_s.at[grp], csend.at[0], crecv.at[0], grp=other_y)
    cot_core = remote(cot, cot_s.at[grp], csend.at[1], crecv.at[1], grp=other_core)
    cot_y.start()
    cot_core.start()
    cot_own = pltpu.make_async_copy(cot, cot_s.at[grp], clocal.at[0])
    cot_own.start()

    def ends(kind, at):
        cols = head_cols(head_at(at, idle))
        if kind == 0:
            return k.at[:, cols], k16.at[z + 4]
        if kind == 1:
            return v.at[:, cols], v16.at[z + 4]
        if kind == 2:
            return q.at[:, cols], q8.at[z]
        if kind == 3:
            return g_loc.at[head_at(at, idle)], g8.at[z]
        return nb_o, nb_v.at[z]

    def send(kind, at):
        src, dst = ends(kind, at)
        return remote(src, dst, ssem.at[kind, at], rsem.at[kind, z], tile=base + at)

    def keep(kind):
        src, dst = ends(kind, z)
        return pltpu.make_async_copy(src, dst, lsem.at[kind])

    def arrived(kind, at):
        dst = (k16.at[at + 4], v16.at[at + 4], q8.at[at], g8.at[at], nb_v.at[at])[kind]
        return remote(dst, dst, ssem.at[kind, 0], rsem.at[kind, at], tile=base + at)

    def send_kinds(kinds):
        @pl.loop(1, RING)
        def _(s):
            at = (z + s) % RING

            @pl.when(owns(at, idle))
            def _():
                for kind in kinds:
                    send(kind, at).start()

        @pl.when(mine)
        def _():
            for kind in kinds:
                keep(kind).start()

    down = lax.broadcasted_iota(jnp.int32, (8, 128), 0)
    across = lax.broadcasted_iota(jnp.int32, (8, 128), 1)
    table = jnp.zeros((8, 128), jnp.int32)
    ids = [listed[0, j] for j in range(NB)]
    for j, n in enumerate(ids):
        near = jnp.where(n >= 0, n - ring * RING + 4, z + 4)
        near = jnp.clip(near, 0, 2 * RING - 1)
        table = jnp.where((down == 0) & (across == j), near, table)
        alive = jnp.where(n >= 0, tokens[jnp.maximum(n, 0)], 0)
        table = jnp.where((down == 1) & (across == j), alive, table)
    for c, (dt, dh) in enumerate(SHIFTS):
        slot = jnp.int32(NB)
        for j in range(1, NB):
            hit = (ids[j] >= 0) & (ids[j] == tile + dt * 4 + dh)
            slot = slot - jnp.where(hit, NB - j, 0)
        table = jnp.where((down == 2) & (across == c), jnp.maximum(slot, 0), table)
    nb_o[...] = table

    send_kinds((4, 0))
    send_kinds((2,))

    remote(cot, cot_s.at[other_y], csend.at[0], crecv.at[0], grp=other_y).wait_recv()
    cot_on = remote(cot_s.at[other_y], cot_s.at[other_y], csend.at[2], crecv.at[2], grp=other_core)
    cot_on.start()
    far = (other_core + 2) % GRP
    remote(cot, cot_s.at[other_core], csend.at[1], crecv.at[1], grp=other_core).wait_recv()
    remote(cot, cot_s.at[far], csend.at[2], crecv.at[2], grp=other_core).wait_recv()
    cot_own.wait()

    @pl.loop(0, HEADS)
    def _(h):
        total = None
        for b in range(GRP):
            part = nt(cot_s[b], w[head_cols(h), b * DBLK:(b + 1) * DBLK])
            total = part if total is None else total + part
        g_loc[h] = total.astype(BF16)

    send_kinds((1,))
    send_kinds((3,))

    def hop(kind, at, start):
        buf = (k16, v16)[kind]

        def go(c):
            if start:
                c.start()
            else:
                c.wait_send()

        @pl.when((at >= 4) & has_up)
        def _():
            go(remote(buf.at[at + 4], buf.at[at - 4], khsend.at[kind, at], khrecv.at[kind, at],
                      tile=tile + RING))

        @pl.when((at < 4) & has_down)
        def _():
            go(remote(buf.at[at + 4], buf.at[at + 12], khsend.at[kind, at], khrecv.at[kind, at],
                      tile=tile - RING))

    def hops_arrived(kind):
        buf = (k16, v16)[kind]

        @pl.loop(0, RING)
        def _(at):
            @pl.when((at >= 4) & has_down)
            def _():
                remote(buf.at[at - 4], buf.at[at - 4], khsend.at[kind, at], khrecv.at[kind, at],
                       tile=tile - RING).wait_recv()

            @pl.when((at < 4) & has_up)
            def _():
                remote(buf.at[at + 12], buf.at[at + 12], khsend.at[kind, at], khrecv.at[kind, at],
                       tile=tile + RING).wait_recv()

    def back_ends(kind, at, h):
        src = (att8, dq8, dkb, dvb)[kind].at[at]
        dst = (att_s, dq, dk, dv)[kind].at[:, head_cols(h)]
        return src, dst

    def back(kind, at):
        src, dst = back_ends(kind, at, my_head)
        return remote(src, dst, osend.at[kind, at], orecv.at[kind, my_head], tile=base + at)

    def back_own(kind):
        src, dst = back_ends(kind, z, my_head)
        return pltpu.make_async_copy(src, dst, olocal.at[kind])

    def back_start(kind, at):
        @pl.when(at != z)
        def _():
            back(kind, at).start()

        @pl.when(at == z)
        def _():
            back_own(kind).start()

    def back_arrived(kind):
        @pl.loop(0, HEADS)
        def _(h):
            at = place_of(h, idle)
            src, dst = back_ends(kind, z, h)

            @pl.when(at != z)
            def _():
                remote(src, dst, osend.at[kind, 0], orecv.at[kind, h], tile=base + at).wait_recv()

        @pl.when(mine)
        def _():
            back_own(kind).wait()

    def local(r, j):
        return nb_s[r, 0, j]

    def count(r, j):
        return nb_s[r, 1, j]

    def gather(acc, r):
        acc[r + 5] += tmp[0]
        for n, (dt, dh) in enumerate(SHIFTS):
            acc[r + 5 + dt * 4 + dh] += tmp[nb_s[r, 2, n]]

    def weigh(r):
        queries = q8[r]
        rows = lax.broadcasted_iota(jnp.int32, (TILE, TILE), 0)
        top = jnp.full((8, TILE), -1e30, F32)
        for j in range(NB):
            s = nt(k16[local(r, j)], queries)
            s = jnp.where(rows < count(r, j), s, F32(-1e30))
            s_scr[j * TILE:(j + 1) * TILE, :] = s
            top = jnp.maximum(top, jnp.max(s.reshape(TILE // 8, 8, TILE), axis=0))
        top = jnp.max(top, axis=0, keepdims=True)
        total = jnp.zeros((8, TILE), F32)
        for j in range(NB):
            e = jnp.exp2((s_scr[j * TILE:(j + 1) * TILE, :] - top) * F32(FACTOR * LOG2E))
            s_scr[j * TILE:(j + 1) * TILE, :] = e
            total = total + jnp.sum(e.reshape(TILE // 8, 8, TILE), axis=0)
        inverse = 1.0 / jnp.sum(total, axis=0, keepdims=True)
        for j in range(NB):
            p[r, j * TILE:(j + 1) * TILE, :] = (
                s_scr[j * TILE:(j + 1) * TILE, :] * inverse
            ).astype(BF16)

    def attend(r):
        for j in range(NB):
            vc[j * TILE:(j + 1) * TILE, :] = v16[local(r, j)]
        out = tn(vc[...], p[r])
        o_t[r] = out
        att8[r] = out.T.astype(BF16)

    def value_part(r):
        tmp[0:NB] = jnp.dot(p[r], g8[r], preferred_element_type=F32).reshape(NB, TILE, HEAD_DIM)
        gather(accv, r)

    def score_part(r):
        grads = g8[r]
        delta = jnp.sum(o_t[r] * grads.astype(F32).T, axis=0, keepdims=True)
        for j in range(NB):
            rows = slice(j * TILE, (j + 1) * TILE)
            at = local(r, j)
            gp = nt(v16[at], grads)
            ds_s[rows, :] = (p[r, rows, :].astype(F32) * ((gp - delta) * F32(FACTOR))).astype(BF16)
            kc[rows, :] = k16[at]
        keys = jnp.dot(ds_s[...], q8[r], preferred_element_type=F32)
        tmp[0:NB] = keys.reshape(NB, TILE, HEAD_DIM)
        dq8[r] = tn(kc[...], ds_s[...]).T.astype(BF16)
        gather(acck, r)

    def halo(kind, up):
        src, dst = ((hks, hk), (hvs, hv))[kind]
        if up:
            return remote(src.at[pl.ds(4, 4)], dst.at[pl.ds(0, 4)], hsend.at[kind, 1],
                          hrecv.at[kind, 0], tile=tile + RING)
        return remote(src.at[pl.ds(0, 4)], dst.at[pl.ds(4, 4)], hsend.at[kind, 0],
                      hrecv.at[kind, 1], tile=tile - RING)

    def halo_start(kind):
        acc, src = ((acck, hks), (accv, hvs))[kind]

        @pl.when(has_down)
        def _():
            @pl.loop(0, 4)
            def _(i):
                src[i] = acc[i + 1].astype(BF16)
            halo(kind, False).start()

        @pl.when(has_up)
        def _():
            @pl.loop(0, 4)
            def _(i):
                src[i + 4] = acc[i + 13].astype(BF16)
            halo(kind, True).start()

    def home(kind):
        acc, got, out = ((acck, hk, dkb), (accv, hv, dvb))[kind]

        @pl.when(has_down)
        def _():
            halo(kind, True).wait_recv()

        @pl.when(has_up)
        def _():
            halo(kind, False).wait_recv()

        @pl.loop(0, RING)
        def _(s):
            at = (z + s) % RING
            given = ((at < 4) & has_down) | ((at >= 4) & has_up)

            @pl.when(given)
            def _():
                out[at] = (acc[at + 5] + got[at].astype(F32)).astype(BF16)

            @pl.when(jnp.logical_not(given))
            def _():
                out[at] = acc[at + 5].astype(BF16)

            back_start(2 + kind, at)

    def blk(i, size):
        return pl.ds(pl.multiple_of(i % 4 * size, size), size)

    class Line:
        def __init__(self, src, first, size, land, stage, slot):
            a, b = pl.ds(first, QUARTER), pl.ds(first + QUARTER, QUARTER)
            self.src, self.cols, self.size, self.land, self.stage = src, (a, b), size, land, stage

            def leg(i, col, n, to):
                return remote(src.at[blk(i, size), col], land.at[n], xsend.at[slot + n],
                              xrecv.at[slot + n], tile=to)

            self.rel = (leg(x + 2, a, 0, left), leg(x + 2, b, 1, right))
            self.one = (leg(x + 1, a, 2, right), leg(x + 3, b, 3, left))
            self.sum = tuple(
                remote(stage.at[n], land.at[4 + n], xsend.at[slot + 4 + n], xrecv.at[slot + 4 + n],
                       tile=(left, right)[n])
                for n in range(2)
            )

        def start(self):
            for c in self.rel + self.one:
                c.start()

        def relay(self):
            for n in range(2):
                self.rel[n].wait_recv()
                mine_too = self.src[blk(x + (3, 1)[n], self.size), self.cols[n]]
                self.stage[n] = (self.land[n].astype(F32) + mine_too.astype(F32)).astype(BF16)
                self.sum[n].start()

        def total(self, n):
            self.one[n].wait_recv()
            self.sum[n].wait_recv()
            here = self.src[blk(x, self.size), self.cols[n]]
            return here.astype(F32) + self.land[2 + n].astype(F32) + self.land[4 + n].astype(F32)

        def sent(self):
            for c in self.rel + self.one + self.sum:
                c.wait_send()

    first = Line(dwp, 0, XROWS, x1, xs1, 0)
    second = Line(y2, 0, SROWS, x2, xs2, 6)

    def half_rows(i):
        return pl.ds(pl.multiple_of(i * YROWS, YROWS), YROWS)

    y2_send = remote(dwp.at[half_rows(1 - y), pl.ds(HALF, HALF)], y2l, ysend.at[0], yrecv.at[0],
                     tile=y_pair)
    y1_send = remote(y1s, y1l, ysend.at[1], yrecv.at[1], tile=y_pair)
    to_core = remote(pos, pol, gsend.at[0], grecv.at[0], grp=other_core)
    to_y = remote(ybs, ybl, gsend.at[1], grecv.at[1], grp=other_y)

    def projected(b):
        cols = pl.ds(pl.multiple_of(b * DBLK, DBLK), DBLK)
        return jnp.dot(att_s[...], w[:, cols], preferred_element_type=F32)

    def stage_1():
        back_arrived(0)

        @pl.loop(0, HEADS)
        def _(h):
            rows = head_cols(h)
            turned = att_s[:, rows].T
            for b in range(GRP):
                dwp[rows, b * DBLK:(b + 1) * DBLK] = jnp.dot(
                    turned, cot_s[b], preferred_element_type=F32
                ).astype(BF16)

        y2_send.start()
        first.start()

        @pl.loop(0, 2)
        def _(yy):
            pos[yy] = projected(yy * 2 + 1 - core)

        to_core.start()

        @pl.loop(0, 2)
        def _(yy):
            own[yy] = projected(yy * 2 + core)

    def stage_2():
        first.relay()

    def stage_3():
        y2_send.wait_recv()
        y2[...] = (
            dwp[half_rows(y), HALF:].astype(F32) + y2l[...].astype(F32)
        ).astype(BF16)
        second.start()
        to_core.wait_recv()
        ybs[...] = (own[1 - y_hi] + pol[1 - y_hi]).astype(BF16)
        to_y.start()

    def mid_rows(i):
        return pl.ds(pl.multiple_of(i * SROWS, SROWS), SROWS)

    def stage_4():
        for n in range(2):
            cols = slice(n * QUARTER, (n + 1) * QUARTER)
            total = first.total(n)
            x_tot[n] = total
            y1s[:, cols] = x_tot[n, mid_rows(1 - y), :].astype(BF16)
        y1_send.start()
        second.relay()

    def stage_5():
        for n in range(2):
            zs[:, HALF + n * QUARTER:HALF + (n + 1) * QUARTER] = second.total(n).astype(BF16)
        y1_send.wait_recv()
        for n in range(2):
            cols = slice(n * QUARTER, (n + 1) * QUARTER)
            zs[:, cols] = (x_tot[n, mid_rows(y), :] + y1l[:, cols].astype(F32)).astype(BF16)

        @pl.loop(1, RING)
        def _(s):
            z_sum(s).start()

    def zpart(at):
        return (
            pl.ds(pl.multiple_of(at // 4 * ZROWS, ZROWS), ZROWS),
            pl.ds(pl.multiple_of(at % 4 * ZCOLS, ZCOLS), ZCOLS),
        )

    def z_sum(s):
        at = (z + s) % RING
        return remote(zs.at[zpart(at)], zl.at[z], zsend.at[0, s], zrecv.at[0, z], tile=base + at)

    def finished(at):
        row = jnp.where(at % 4 < 2, x * XROWS + y * SROWS, y * YROWS + x * SROWS)
        rows = pl.ds(pl.multiple_of(row + at // 4 * ZROWS, ZROWS), ZROWS)
        return dw.at[rows, zpart(at)[1]]

    def z_all(s):
        at = (z + s) % RING
        return remote(fin, finished(z), zsend.at[1, s], zrecv.at[1, z], tile=base + at)

    fin_own = pltpu.make_async_copy(fin, finished(z), olocal.at[4])

    def stage_6():
        rows, cols = zpart(z)
        total = zs[rows, cols].astype(F32)
        for s in range(1, RING):
            at = (z + s) % RING
            remote(zl.at[at], zl.at[at], zsend.at[0, 0], zrecv.at[0, at], tile=base + at).wait_recv()
            total += zl[at].astype(F32)
        fin[...] = total.astype(BF16)

        @pl.loop(1, RING)
        def _(s):
            z_all(s).start()

        fin_own.start()

    lo, hi = pl.ds(0, HALF), pl.ds(HALF, HALF)

    def slab_1y(yy):
        return dw.at[pl.ds(pl.multiple_of(x * XROWS + yy * SROWS, SROWS), SROWS), lo]

    def slab_2y(yy):
        return dw.at[half_rows(yy), hi]

    all_1y = remote(slab_1y(y), slab_1y(y), ysend.at[2], yrecv.at[2], tile=y_pair)
    got_1y = remote(slab_1y(1 - y), slab_1y(1 - y), ysend.at[2], yrecv.at[2], tile=y_pair)
    all_2y = remote(slab_2y(y), slab_2y(y), ysend.at[3], yrecv.at[3], tile=y_pair)
    got_2y = remote(slab_2y(1 - y), slab_2y(1 - y), ysend.at[3], yrecv.at[3], tile=y_pair)

    class Spread:
        def __init__(self, rows, cols, slot):
            def part(i, n, k, to):
                ref = dw.at[rows(i), pl.ds(cols + n * QUARTER, QUARTER)]
                return remote(ref, ref, xsend.at[slot + k], xrecv.at[slot + k], tile=to)

            self.outs = (
                part(x, 0, 0, right), part(x, 1, 1, left), part(x, 1, 2, right), part(x, 0, 3, left)
            )
            self.near = (part(x + 3, 0, 0, left), part(x + 1, 1, 1, right))
            self.on = (part(x + 3, 0, 4, right), part(x + 1, 1, 5, left))
            self.rest = (
                part(x + 3, 1, 2, left), part(x + 1, 0, 3, right),
                part(x + 2, 0, 4, left), part(x + 2, 1, 5, right),
            )

        def start(self):
            for c in self.outs:
                c.start()

        def relay(self):
            for n in range(2):
                self.near[n].wait_recv()
                self.on[n].start()

        def finish(self):
            for c in self.rest:
                c.wait_recv()

        def sent(self):
            for c in self.outs + self.on:
                c.wait_send()

    spread_1 = Spread(lambda i: blk(i, XROWS), 0, 12)
    spread_2 = Spread(
        lambda i: pl.ds(pl.multiple_of(y * YROWS + i % 4 * SROWS, SROWS), SROWS), HALF, 18
    )

    def stage_7():
        @pl.loop(1, RING)
        def _(s):
            at = (z + s) % RING
            remote(fin, finished(at), zsend.at[1, 0], zrecv.at[1, at], tile=base + at).wait_recv()

        fin_own.wait()
        spread_2.start()
        all_1y.start()

    def stage_8():
        to_y.wait_recv()
        bo[...] = (own[y_hi] + pol[y_hi] + ybl[...].astype(F32)).astype(BF16)
        spread_2.relay()
        got_1y.wait_recv()
        spread_1.start()
        spread_2.finish()
        all_2y.start()
        spread_1.relay()
        got_2y.wait_recv()
        spread_1.finish()

    @pl.when(mine)
    def _():
        acck[...] = jnp.zeros_like(acck)
        accv[...] = jnp.zeros_like(accv)
        tmp[NB] = jnp.zeros((TILE, HEAD_DIM), F32)
        keep(0).wait()
        hop(0, z, True)

        @pl.loop(1, RING)
        def _(s):
            at = (z + RING - s) % RING
            arrived(0, at).wait_recv()
            hop(0, at, True)

        for kind in (2, 4):
            keep(kind).wait()

            @pl.loop(1, RING)
            def _(s):
                arrived(kind, (z + s) % RING).wait_recv()

        lists = pltpu.make_async_copy(nb_v, nb_s, lsem.at[5])
        lists.start()
        hops_arrived(0)
        lists.wait()

        @pl.loop(0, RING)
        def _(i):
            weigh((z + i) % RING)

            @pl.when(i == 0)
            def _():
                keep(1).wait()
                hop(1, z, True)

            @pl.when(i > 0)
            def _():
                at = (z + RING - i) % RING
                arrived(1, at).wait_recv()
                hop(1, at, True)

        hops_arrived(1)

        @pl.loop(0, RING)
        def _(i):
            r = (z + i) % RING
            attend(r)
            back_start(0, r)

        keep(3).wait()

        @pl.loop(1, RING)
        def _(s):
            arrived(3, (z + s) % RING).wait_recv()

        @pl.loop(0, RING)
        def _(i):
            value_part((z + i) % RING)

        halo_start(1)

    stage_1()

    @pl.loop(0, RING)
    def _(i):
        @pl.when(mine)
        def _():
            r = (z + i) % RING
            score_part(r)
            back_start(1, r)

            @pl.when(i == 2)
            def _():
                home(1)

        @pl.when(i == 3)
        def _():
            stage_2()

        @pl.when(i == 5)
        def _():
            stage_3()

    @pl.when(mine)
    def _():
        halo_start(0)

    stage_4()

    @pl.when(mine)
    def _():
        home(0)

    stage_5()
    stage_6()
    stage_7()
    stage_8()

    for kind in (1, 2, 3):
        back_arrived(kind)

    @pl.loop(1, RING)
    def _(s):
        at = (z + s) % RING

        @pl.when(owns(at, idle))
        def _():
            for kind in range(5):
                send(kind, at).wait_send()

        @pl.when(mine)
        def _():
            for kind in range(4):
                back(kind, at).wait_send()

        z_sum(s).wait_send()
        z_all(s).wait_send()

    @pl.when(mine)
    def _():
        @pl.loop(0, RING)
        def _(at):
            for kind in (0, 1):
                hop(kind, at, False)

        for kind in (0, 1):
            @pl.when(has_down)
            def _():
                halo(kind, False).wait_send()

            @pl.when(has_up)
            def _():
                halo(kind, True).wait_send()

    for c in (cot_y, cot_core, cot_on, y2_send, y1_send, to_core, to_y, all_1y, all_2y):
        c.wait_send()
    for c in (first, second, spread_1, spread_2):
        c.sent()


def step(listed, tokens, q, k, v, cot, w):
    any_space = pl.BlockSpec(memory_space=pl.ANY)
    vmem = pl.BlockSpec(memory_space=pltpu.VMEM)
    smem = pl.BlockSpec(memory_space=pltpu.SMEM)
    dma = pltpu.SemaphoreType.DMA
    grad = jax.ShapeDtypeStruct((TILE, FEAT), BF16)

    def tiles(n, dtype=BF16):
        return pltpu.VMEM((n, TILE, HEAD_DIM), dtype)

    return pl.pallas_call(
        step_kernel,
        out_shape=(
            jax.ShapeDtypeStruct((TILE, DBLK), BF16), grad, grad, grad,
            jax.ShapeDtypeStruct((FEAT, DOUT), BF16),
        ),
        in_specs=[smem, smem, any_space, any_space, any_space, vmem, vmem],
        out_specs=(vmem, any_space, any_space, any_space, any_space),
        scratch_shapes=[
            pltpu.VMEM((8, 128), jnp.int32),
            pltpu.VMEM((RING, 8, 128), jnp.int32),
            pltpu.SMEM((RING, 8, 128), jnp.int32),
            tiles(2 * RING),
            tiles(2 * RING),
            tiles(RING),
            tiles(RING),
            pltpu.VMEM((GRP, TILE, DBLK), BF16),
            tiles(HEADS),
            pltpu.VMEM((KEYS, TILE), F32),
            pltpu.VMEM((RING, KEYS, TILE), BF16),
            pltpu.VMEM((KEYS, HEAD_DIM), BF16),
            pltpu.VMEM((KEYS, HEAD_DIM), BF16),
            pltpu.VMEM((KEYS, TILE), BF16),
            tiles(NB + 1, F32),
            pltpu.VMEM((RING, HEAD_DIM, TILE), F32),
            tiles(2 * RING + 2, F32),
            tiles(2 * RING + 2, F32),
            tiles(RING),
            tiles(RING),
            pltpu.VMEM((TILE, FEAT), BF16),
            tiles(RING),
            tiles(RING),
            tiles(RING),
            tiles(RING),
            tiles(RING),
            tiles(RING),
            pltpu.VMEM((FEAT, DOUT), BF16),
            pltpu.VMEM((6, XROWS, QUARTER), BF16),
            pltpu.VMEM((6, SROWS, QUARTER), BF16),
            pltpu.VMEM((2, XROWS, QUARTER), BF16),
            pltpu.VMEM((2, SROWS, QUARTER), BF16),
            pltpu.VMEM((2, XROWS, QUARTER), F32),
            pltpu.VMEM((SROWS, HALF), BF16),
            pltpu.VMEM((SROWS, HALF), BF16),
            pltpu.VMEM((YROWS, HALF), BF16),
            pltpu.VMEM((YROWS, HALF), BF16),
            pltpu.VMEM((SROWS, DOUT), BF16),
            pltpu.VMEM((RING, ZROWS, ZCOLS), BF16),
            pltpu.VMEM((ZROWS, ZCOLS), BF16),
            pltpu.VMEM((2, TILE, DBLK), F32),
            pltpu.VMEM((2, TILE, DBLK), F32),
            pltpu.VMEM((2, TILE, DBLK), F32),
            pltpu.VMEM((TILE, DBLK), BF16),
            pltpu.VMEM((TILE, DBLK), BF16),
            dma((5, RING)),
            dma((5, RING)),
            dma((6,)),
            dma((3,)),
            dma((3,)),
            dma((1,)),
            dma((2, RING)),
            dma((2, RING)),
            dma((4, RING)),
            dma((4, HEADS)),
            dma((5,)),
            dma((2, 2)),
            dma((2, 2)),
            dma((24,)),
            dma((24,)),
            dma((4,)),
            dma((4,)),
            dma((2, RING)),
            dma((2, RING)),
            dma((2,)),
            dma((2,)),
        ],
        compiler_params=pltpu.CompilerParams(
            collective_id=0, has_side_effects=True, vmem_limit_bytes=VMEM_LIMIT
        ),
        name="step",
    )(listed, tokens, q, k, v, cot, w)


def body(query_tokens, key_tokens, value_tokens, w_out, cotangent, neighbours, tile_tokens):
    return step(
        neighbours, tile_tokens, query_tokens, key_tokens, value_tokens, cotangent, w_out
    )


def solution(mesh):
    placed = (
        P("tile", "grp"),
        P("tile", "grp"),
        P("tile", "grp"),
        P("grp", None),
        P("tile", "grp"),
        P("tile", None),
        P(),
    )
    return jax.shard_map(
        body,
        mesh=mesh,
        in_specs=placed,
        out_specs=(
            P("tile", "grp"),
            P("tile", "grp"),
            P("tile", "grp"),
            P("tile", "grp"),
            P("grp", None),
        ),
        check_vma=False,
    )
```

```python
import math

import jax
import jax.numpy as jnp
from jax import lax
from jax.experimental import pallas as pl
from jax.experimental.pallas import tpu as pltpu
from jax.sharding import PartitionSpec as P

MESH = pl.DeviceIdType.MESH
HEAD_DIM = 128
TILE = 384
NB = 5
HEADS = 6
RING = 8
RINGS = 8
FEAT = HEADS * HEAD_DIM
GRP = 4
DBLK = 384
DOUT = GRP * DBLK
FACTOR = 1.0 / math.sqrt(HEAD_DIM)
BF16 = jnp.bfloat16
F32 = jnp.float32
VMEM_LIMIT = 56 * 1024 * 1024


def whereabouts():
    tile = lax.axis_index("tile")
    grp = lax.axis_index("grp")
    z = tile % RING
    ring = tile // RING
    core = grp % 2
    idle = 3 - 2 * core
    return tile, grp, z, ring, core, idle


def owns(z, idle):
    return z % 4 != idle


def head_at(z, idle):
    zz = z % 4
    return (z // 4) * 3 + zz - jnp.where(zz > idle, 1, 0)


def place_of(head, idle):
    hh = head % 3
    return (head // 3) * 4 + hh + jnp.where(hh >= idle, 1, 0)


def head_cols(head):
    return pl.ds(pl.multiple_of(head * HEAD_DIM, HEAD_DIM), HEAD_DIM)


def remote(src, dst, send_sem, recv_sem, **where):
    return pltpu.make_async_remote_copy(
        src_ref=src,
        dst_ref=dst,
        send_sem=send_sem,
        recv_sem=recv_sem,
        device_id=where,
        device_id_type=MESH,
    )


def signal(barrier, **where):
    pl.semaphore_signal(barrier, inc=1, device_id=where, device_id_type=MESH)


def greet_ring(barrier, tile, z, ring):
    @pl.loop(1, RING)
    def _(s):
        signal(barrier, tile=tile - z + (z + s) % RING)

    @pl.when(ring > 0)
    def _():
        signal(barrier, tile=tile - RING)

    @pl.when(ring < RINGS - 1)
    def _():
        signal(barrier, tile=tile + RING)


def ring_edges(ring):
    return jnp.where(ring > 0, 1, 0) + jnp.where(ring < RINGS - 1, 1, 0)

XROWS = FEAT // 4
YROWS = FEAT // 2
SROWS = FEAT // 8
ZROWS = SROWS // 2
ZCOLS = DOUT // 4
HALF = DOUT // 2
QUARTER = DOUT // 4
KEYS = NB * TILE
SHIFTS = tuple((dt, dh) for dt in (-1, 0, 1) for dh in (-1, 0, 1) if (dt, dh) != (0, 0))
LOG2E = math.log2(math.e)


def nt(a, b):
    return lax.dot_general(a, b, (((1,), (1,)), ((), ())), preferred_element_type=F32)


def tn(a, b):
    return lax.dot_general(a, b, (((0,), (0,)), ((), ())), preferred_element_type=F32)


def step_kernel(
    listed, tokens, q, k, v, cot, w,
    bo, dq, dk, dv, dw,
    nb_o, nb_v, nb_s, k16, v16, q8, g8, cot_s, g_loc, s_scr, p, vc, tmp, o_t, acck, accv,
    att8, dq8, att_s, hk, hv, hks, hvs, dkb, dvb,
    dwp, x1, x2, xs1, xs2, x_tot, y1s, y1l, y2l, y2, zs, zl, fin, pos, pol, own, ybs, ybl,
    ssem, rsem, lsem, csend, crecv, clocal, khsend, khrecv, osend, orecv, olocal, hsend, hrecv,
    xsend, xrecv, ysend, yrecv, zsend, zrecv, gsend, grecv,
):
    tile, grp, z, ring, core, idle = whereabouts()
    base = tile - z
    mine = owns(z, idle)
    my_head = head_at(z, idle)
    x = ring % 4
    y = ring // 4
    right = tile - x * RING + (x + 1) % 4 * RING
    left = tile - x * RING + (x + 3) % 4 * RING
    y_pair = tile + 32 - 64 * y
    other_core = grp + 1 - 2 * core
    other_y = (grp + 2) % GRP
    y_hi = grp // 2
    has_up = ring < RINGS - 1
    has_down = ring > 0

    barrier = pltpu.get_barrier_semaphore()
    greet_ring(barrier, tile, z, ring)
    for where in (right, left, y_pair):
        signal(barrier, tile=where)
    signal(barrier, grp=other_core)
    signal(barrier, grp=other_y)
    pl.semaphore_wait(barrier, RING - 1 + 5 + ring_edges(ring))

    cot_y = remote(cot, cot_s.at[grp], csend.at[0], crecv.at[0], grp=other_y)
    cot_core = remote(cot, cot_s.at[grp], csend.at[1], crecv.at[1], grp=other_core)
    cot_y.start()
    cot_core.start()
    cot_own = pltpu.make_async_copy(cot, cot_s.at[grp], clocal.at[0])
    cot_own.start()

    def ends(kind, at):
        cols = head_cols(head_at(at, idle))
        if kind == 0:
            return k.at[:, cols], k16.at[z + 4]
        if kind == 1:
            return v.at[:, cols], v16.at[z + 4]
        if kind == 2:
            return q.at[:, cols], q8.at[z]
        if kind == 3:
            return g_loc.at[head_at(at, idle)], g8.at[z]
        return nb_o, nb_v.at[z]

    def send(kind, at):
        src, dst = ends(kind, at)
        return remote(src, dst, ssem.at[kind, at], rsem.at[kind, z], tile=base + at)

    def keep(kind):
        src, dst = ends(kind, z)
        return pltpu.make_async_copy(src, dst, lsem.at[kind])

    def arrived(kind, at):
        dst = (k16.at[at + 4], v16.at[at + 4], q8.at[at], g8.at[at], nb_v.at[at])[kind]
        return remote(dst, dst, ssem.at[kind, 0], rsem.at[kind, at], tile=base + at)

    def send_kinds(kinds):
        @pl.loop(1, RING)
        def _(s):
            at = (z + s) % RING

            @pl.when(owns(at, idle))
            def _():
                for kind in kinds:
                    send(kind, at).start()

        @pl.when(mine)
        def _():
            for kind in kinds:
                keep(kind).start()

    down = lax.broadcasted_iota(jnp.int32, (8, 128), 0)
    across = lax.broadcasted_iota(jnp.int32, (8, 128), 1)
    table = jnp.zeros((8, 128), jnp.int32)
    ids = [listed[0, j] for j in range(NB)]
    for j, n in enumerate(ids):
        near = jnp.where(n >= 0, n - ring * RING + 4, z + 4)
        near = jnp.clip(near, 0, 2 * RING - 1)
        table = jnp.where((down == 0) & (across == j), near, table)
        alive = jnp.where(n >= 0, tokens[jnp.maximum(n, 0)], 0)
        table = jnp.where((down == 1) & (across == j), alive, table)
    for c, (dt, dh) in enumerate(SHIFTS):
        slot = jnp.int32(NB)
        for j in range(1, NB):
            hit = (ids[j] >= 0) & (ids[j] == tile + dt * 4 + dh)
            slot = slot - jnp.where(hit, NB - j, 0)
        table = jnp.where((down == 2) & (across == c), jnp.maximum(slot, 0), table)
    nb_o[...] = table

    send_kinds((4, 0))
    send_kinds((2,))

    remote(cot, cot_s.at[other_y], csend.at[0], crecv.at[0], grp=other_y).wait_recv()
    cot_on = remote(cot_s.at[other_y], cot_s.at[other_y], csend.at[2], crecv.at[2], grp=other_core)
    cot_on.start()
    far = (other_core + 2) % GRP
    remote(cot, cot_s.at[other_core], csend.at[1], crecv.at[1], grp=other_core).wait_recv()
    remote(cot, cot_s.at[far], csend.at[2], crecv.at[2], grp=other_core).wait_recv()
    cot_own.wait()

    @pl.loop(0, HEADS)
    def _(h):
        total = None
        for b in range(GRP):
            part = nt(cot_s[b], w[head_cols(h), b * DBLK:(b + 1) * DBLK])
            total = part if total is None else total + part
        g_loc[h] = total.astype(BF16)

    send_kinds((1,))
    send_kinds((3,))

    def hop(kind, at, start):
        buf = (k16, v16)[kind]

        def go(c):
            if start:
                c.start()
            else:
                c.wait_send()

        @pl.when((at >= 4) & has_up)
        def _():
            go(remote(buf.at[at + 4], buf.at[at - 4], khsend.at[kind, at], khrecv.at[kind, at],
                      tile=tile + RING))

        @pl.when((at < 4) & has_down)
        def _():
            go(remote(buf.at[at + 4], buf.at[at + 12], khsend.at[kind, at], khrecv.at[kind, at],
                      tile=tile - RING))

    def hops_arrived(kind):
        buf = (k16, v16)[kind]

        @pl.loop(0, RING)
        def _(at):
            @pl.when((at >= 4) & has_down)
            def _():
                remote(buf.at[at - 4], buf.at[at - 4], khsend.at[kind, at], khrecv.at[kind, at],
                       tile=tile - RING).wait_recv()

            @pl.when((at < 4) & has_up)
            def _():
                remote(buf.at[at + 12], buf.at[at + 12], khsend.at[kind, at], khrecv.at[kind, at],
                       tile=tile + RING).wait_recv()

    def back_ends(kind, at, h):
        src = (att8, dq8, dkb, dvb)[kind].at[at]
        dst = (att_s, dq, dk, dv)[kind].at[:, head_cols(h)]
        return src, dst

    def back(kind, at):
        src, dst = back_ends(kind, at, my_head)
        return remote(src, dst, osend.at[kind, at], orecv.at[kind, my_head], tile=base + at)

    def back_own(kind):
        src, dst = back_ends(kind, z, my_head)
        return pltpu.make_async_copy(src, dst, olocal.at[kind])

    def back_start(kind, at):
        @pl.when(at != z)
        def _():
            back(kind, at).start()

        @pl.when(at == z)
        def _():
            back_own(kind).start()

    def back_arrived(kind):
        @pl.loop(0, HEADS)
        def _(h):
            at = place_of(h, idle)
            src, dst = back_ends(kind, z, h)

            @pl.when(at != z)
            def _():
                remote(src, dst, osend.at[kind, 0], orecv.at[kind, h], tile=base + at).wait_recv()

        @pl.when(mine)
        def _():
            back_own(kind).wait()

    def local(r, j):
        return nb_s[r, 0, j]

    def count(r, j):
        return nb_s[r, 1, j]

    def gather(acc, r):
        acc[r + 5] += tmp[0]
        for n, (dt, dh) in enumerate(SHIFTS):
            acc[r + 5 + dt * 4 + dh] += tmp[nb_s[r, 2, n]]

    def weigh(r):
        queries = q8[r]
        rows = lax.broadcasted_iota(jnp.int32, (TILE, TILE), 0)
        top = jnp.full((8, TILE), -1e30, F32)
        for j in range(NB):
            s = nt(k16[local(r, j)], queries)
            s = jnp.where(rows < count(r, j), s, F32(-1e30))
            s_scr[j * TILE:(j + 1) * TILE, :] = s
            top = jnp.maximum(top, jnp.max(s.reshape(TILE // 8, 8, TILE), axis=0))
        top = jnp.max(top, axis=0, keepdims=True)
        total = jnp.zeros((8, TILE), F32)
        for j in range(NB):
            e = jnp.exp2((s_scr[j * TILE:(j + 1) * TILE, :] - top) * F32(FACTOR * LOG2E))
            s_scr[j * TILE:(j + 1) * TILE, :] = e
            total = total + jnp.sum(e.reshape(TILE // 8, 8, TILE), axis=0)
        inverse = 1.0 / jnp.sum(total, axis=0, keepdims=True)
        for j in range(NB):
            p[r, j * TILE:(j + 1) * TILE, :] = (
                s_scr[j * TILE:(j + 1) * TILE, :] * inverse
            ).astype(BF16)

    def attend(r):
        for j in range(NB):
            vc[j * TILE:(j + 1) * TILE, :] = v16[local(r, j)]
        out = tn(vc[...], p[r])
        o_t[r] = out
        att8[r] = out.T.astype(BF16)

    def value_part(r):
        tmp[0:NB] = jnp.dot(p[r], g8[r], preferred_element_type=F32).reshape(NB, TILE, HEAD_DIM)
        gather(accv, r)

    def key_part(r):
        grads = g8[r]
        delta = jnp.sum(o_t[r] * grads.astype(F32).T, axis=0, keepdims=True)
        for j in range(NB):
            rows = slice(j * TILE, (j + 1) * TILE)
            gp = nt(v16[local(r, j)], grads)
            ds = p[r, rows, :].astype(F32) * ((gp - delta) * F32(FACTOR))
            p[r, rows, :] = ds.astype(BF16)
        keys = jnp.dot(p[r], q8[r], preferred_element_type=F32)
        tmp[0:NB] = keys.reshape(NB, TILE, HEAD_DIM)
        gather(acck, r)

    def query_part(r):
        for j in range(NB):
            vc[j * TILE:(j + 1) * TILE, :] = k16[local(r, j)]
        dq8[r] = tn(vc[...], p[r]).T.astype(BF16)

    def halo(kind, up):
        src, dst = ((hks, hk), (hvs, hv))[kind]
        if up:
            return remote(src.at[pl.ds(4, 4)], dst.at[pl.ds(0, 4)], hsend.at[kind, 1],
                          hrecv.at[kind, 0], tile=tile + RING)
        return remote(src.at[pl.ds(0, 4)], dst.at[pl.ds(4, 4)], hsend.at[kind, 0],
                      hrecv.at[kind, 1], tile=tile - RING)

    def halo_start(kind):
        acc, src = ((acck, hks), (accv, hvs))[kind]

        @pl.when(has_down)
        def _():
            @pl.loop(0, 4)
            def _(i):
                src[i] = acc[i + 1].astype(BF16)
            halo(kind, False).start()

        @pl.when(has_up)
        def _():
            @pl.loop(0, 4)
            def _(i):
                src[i + 4] = acc[i + 13].astype(BF16)
            halo(kind, True).start()

    def home(kind):
        acc, got, out = ((acck, hk, dkb), (accv, hv, dvb))[kind]

        @pl.when(has_down)
        def _():
            halo(kind, True).wait_recv()

        @pl.when(has_up)
        def _():
            halo(kind, False).wait_recv()

        @pl.loop(0, RING)
        def _(s):
            at = (z + s) % RING
            given = ((at < 4) & has_down) | ((at >= 4) & has_up)

            @pl.when(given)
            def _():
                out[at] = (acc[at + 5] + got[at].astype(F32)).astype(BF16)

            @pl.when(jnp.logical_not(given))
            def _():
                out[at] = acc[at + 5].astype(BF16)

            back_start(2 + kind, at)

    def blk(i, size):
        return pl.ds(pl.multiple_of(i % 4 * size, size), size)

    class Line:
        def __init__(self, src, first, size, land, stage, slot):
            a, b = pl.ds(first, QUARTER), pl.ds(first + QUARTER, QUARTER)
            self.src, self.cols, self.size, self.land, self.stage = src, (a, b), size, land, stage

            def leg(i, col, n, to):
                return remote(src.at[blk(i, size), col], land.at[n], xsend.at[slot + n],
                              xrecv.at[slot + n], tile=to)

            self.rel = (leg(x + 2, a, 0, left), leg(x + 2, b, 1, right))
            self.one = (leg(x + 1, a, 2, right), leg(x + 3, b, 3, left))
            self.sum = tuple(
                remote(stage.at[n], land.at[4 + n], xsend.at[slot + 4 + n], xrecv.at[slot + 4 + n],
                       tile=(left, right)[n])
                for n in range(2)
            )

        def start(self):
            for c in self.rel + self.one:
                c.start()

        def relay(self):
            for n in range(2):
                self.rel[n].wait_recv()
                mine_too = self.src[blk(x + (3, 1)[n], self.size), self.cols[n]]
                self.stage[n] = (self.land[n].astype(F32) + mine_too.astype(F32)).astype(BF16)
                self.sum[n].start()

        def total(self, n):
            self.one[n].wait_recv()
            self.sum[n].wait_recv()
            here = self.src[blk(x, self.size), self.cols[n]]
            return here.astype(F32) + self.land[2 + n].astype(F32) + self.land[4 + n].astype(F32)

        def sent(self):
            for c in self.rel + self.one + self.sum:
                c.wait_send()

    first = Line(dwp, 0, XROWS, x1, xs1, 0)
    second = Line(y2, 0, SROWS, x2, xs2, 6)

    def half_rows(i):
        return pl.ds(pl.multiple_of(i * YROWS, YROWS), YROWS)

    y2_send = remote(dwp.at[half_rows(1 - y), pl.ds(HALF, HALF)], y2l, ysend.at[0], yrecv.at[0],
                     tile=y_pair)
    y1_send = remote(y1s, y1l, ysend.at[1], yrecv.at[1], tile=y_pair)
    to_core = remote(pos, pol, gsend.at[0], grecv.at[0], grp=other_core)
    to_y = remote(ybs, ybl, gsend.at[1], grecv.at[1], grp=other_y)

    def projected(b):
        cols = pl.ds(pl.multiple_of(b * DBLK, DBLK), DBLK)
        return jnp.dot(att_s[...], w[:, cols], preferred_element_type=F32)

    def stage_1():
        back_arrived(0)

        @pl.loop(0, HEADS)
        def _(h):
            rows = head_cols(h)
            turned = att_s[:, rows].T
            for b in range(GRP):
                dwp[rows, b * DBLK:(b + 1) * DBLK] = jnp.dot(
                    turned, cot_s[b], preferred_element_type=F32
                ).astype(BF16)

        y2_send.start()
        first.start()

        @pl.loop(0, 2)
        def _(yy):
            pos[yy] = projected(yy * 2 + 1 - core)

        to_core.start()

        @pl.loop(0, 2)
        def _(yy):
            own[yy] = projected(yy * 2 + core)

    def stage_2():
        first.relay()

    def stage_3():
        y2_send.wait_recv()
        y2[...] = (
            dwp[half_rows(y), HALF:].astype(F32) + y2l[...].astype(F32)
        ).astype(BF16)
        second.start()
        to_core.wait_recv()
        ybs[...] = (own[1 - y_hi] + pol[1 - y_hi]).astype(BF16)
        to_y.start()

    def mid_rows(i):
        return pl.ds(pl.multiple_of(i * SROWS, SROWS), SROWS)

    def stage_4():
        for n in range(2):
            cols = slice(n * QUARTER, (n + 1) * QUARTER)
            total = first.total(n)
            x_tot[n] = total
            y1s[:, cols] = x_tot[n, mid_rows(1 - y), :].astype(BF16)
        y1_send.start()
        second.relay()

    def stage_5():
        for n in range(2):
            zs[:, HALF + n * QUARTER:HALF + (n + 1) * QUARTER] = second.total(n).astype(BF16)
        y1_send.wait_recv()
        for n in range(2):
            cols = slice(n * QUARTER, (n + 1) * QUARTER)
            zs[:, cols] = (x_tot[n, mid_rows(y), :] + y1l[:, cols].astype(F32)).astype(BF16)

        @pl.loop(1, RING)
        def _(s):
            z_sum(s).start()

    def zpart(at):
        return (
            pl.ds(pl.multiple_of(at // 4 * ZROWS, ZROWS), ZROWS),
            pl.ds(pl.multiple_of(at % 4 * ZCOLS, ZCOLS), ZCOLS),
        )

    def z_sum(s):
        at = (z + s) % RING
        return remote(zs.at[zpart(at)], zl.at[z], zsend.at[0, s], zrecv.at[0, z], tile=base + at)

    def finished(at):
        row = jnp.where(at % 4 < 2, x * XROWS + y * SROWS, y * YROWS + x * SROWS)
        rows = pl.ds(pl.multiple_of(row + at // 4 * ZROWS, ZROWS), ZROWS)
        return dw.at[rows, zpart(at)[1]]

    def z_all(s):
        at = (z + s) % RING
        return remote(fin, finished(z), zsend.at[1, s], zrecv.at[1, z], tile=base + at)

    fin_own = pltpu.make_async_copy(fin, finished(z), olocal.at[4])

    def stage_6():
        rows, cols = zpart(z)
        total = zs[rows, cols].astype(F32)
        for s in range(1, RING):
            at = (z + s) % RING
            remote(zl.at[at], zl.at[at], zsend.at[0, 0], zrecv.at[0, at], tile=base + at).wait_recv()
            total += zl[at].astype(F32)
        fin[...] = total.astype(BF16)

        @pl.loop(1, RING)
        def _(s):
            z_all(s).start()

        fin_own.start()

    lo, hi = pl.ds(0, HALF), pl.ds(HALF, HALF)

    def slab_1y(yy):
        return dw.at[pl.ds(pl.multiple_of(x * XROWS + yy * SROWS, SROWS), SROWS), lo]

    def slab_2y(yy):
        return dw.at[half_rows(yy), hi]

    all_1y = remote(slab_1y(y), slab_1y(y), ysend.at[2], yrecv.at[2], tile=y_pair)
    got_1y = remote(slab_1y(1 - y), slab_1y(1 - y), ysend.at[2], yrecv.at[2], tile=y_pair)
    all_2y = remote(slab_2y(y), slab_2y(y), ysend.at[3], yrecv.at[3], tile=y_pair)
    got_2y = remote(slab_2y(1 - y), slab_2y(1 - y), ysend.at[3], yrecv.at[3], tile=y_pair)

    class Spread:
        def __init__(self, rows, cols, slot):
            def part(i, n, k, to):
                ref = dw.at[rows(i), pl.ds(cols + n * QUARTER, QUARTER)]
                return remote(ref, ref, xsend.at[slot + k], xrecv.at[slot + k], tile=to)

            self.outs = (
                part(x, 0, 0, right), part(x, 1, 1, left), part(x, 1, 2, right), part(x, 0, 3, left)
            )
            self.near = (part(x + 3, 0, 0, left), part(x + 1, 1, 1, right))
            self.on = (part(x + 3, 0, 4, right), part(x + 1, 1, 5, left))
            self.rest = (
                part(x + 3, 1, 2, left), part(x + 1, 0, 3, right),
                part(x + 2, 0, 4, left), part(x + 2, 1, 5, right),
            )

        def start(self):
            for c in self.outs:
                c.start()

        def relay(self):
            for n in range(2):
                self.near[n].wait_recv()
                self.on[n].start()

        def finish(self):
            for c in self.rest:
                c.wait_recv()

        def sent(self):
            for c in self.outs + self.on:
                c.wait_send()

    spread_1 = Spread(lambda i: blk(i, XROWS), 0, 12)
    spread_2 = Spread(
        lambda i: pl.ds(pl.multiple_of(y * YROWS + i % 4 * SROWS, SROWS), SROWS), HALF, 18
    )

    def stage_7():
        @pl.loop(1, RING)
        def _(s):
            at = (z + s) % RING
            remote(fin, finished(at), zsend.at[1, 0], zrecv.at[1, at], tile=base + at).wait_recv()

        fin_own.wait()
        spread_2.start()
        all_1y.start()

    def stage_8():
        to_y.wait_recv()
        bo[...] = (own[y_hi] + pol[y_hi] + ybl[...].astype(F32)).astype(BF16)
        spread_2.relay()
        got_1y.wait_recv()
        spread_1.start()
        spread_2.finish()
        all_2y.start()
        spread_1.relay()
        got_2y.wait_recv()
        spread_1.finish()

    @pl.when(mine)
    def _():
        acck[...] = jnp.zeros_like(acck)
        accv[...] = jnp.zeros_like(accv)
        tmp[NB] = jnp.zeros((TILE, HEAD_DIM), F32)
        keep(0).wait()
        hop(0, z, True)

        @pl.loop(1, RING)
        def _(s):
            at = (z + RING - s) % RING
            arrived(0, at).wait_recv()
            hop(0, at, True)

        keep(4).wait()

        @pl.loop(1, RING)
        def _(s):
            arrived(4, (z + RING - s) % RING).wait_recv()

        lists = pltpu.make_async_copy(nb_v, nb_s, lsem.at[5])
        lists.start()
        hops_arrived(0)
        lists.wait()

        def ready(kind, i):
            @pl.when(i == 0)
            def _():
                keep(kind).wait()

            @pl.when(i > 0)
            def _():
                arrived(kind, (z + RING - i) % RING).wait_recv()

        @pl.loop(0, RING)
        def _(i):
            ready(2, i)
            weigh((z + RING - i) % RING)

            @pl.when(i >= 4)
            def _():
                for n in range(2):
                    s = (i - 4) * 2 + n
                    ready(1, s)
                    hop(1, (z + RING - s) % RING, True)

        hops_arrived(1)

        @pl.loop(0, RING)
        def _(i):
            r = (z + RING - i) % RING
            attend(r)
            back_start(0, r)

        @pl.loop(0, RING)
        def _(i):
            ready(3, i)
            value_part((z + RING - i) % RING)

        halo_start(1)

    stage_1()

    @pl.loop(0, RING)
    def _(i):
        @pl.when(mine)
        def _():
            key_part((z + i) % RING)

            @pl.when(i == 3)
            def _():
                home(1)

        for n, stage in ((2, stage_2), (4, stage_3), (6, stage_4)):
            pl.when(i == n)(stage)

    @pl.when(mine)
    def _():
        halo_start(0)

    stage_5()

    @pl.loop(0, RING)
    def _(i):
        @pl.when(mine)
        def _():
            r = (z + i) % RING
            query_part(r)
            back_start(1, r)

            @pl.when(i == 5)
            def _():
                home(0)

        for n, stage in ((4, stage_6), (7, stage_7)):
            pl.when(i == n)(stage)

    stage_8()

    for kind in (1, 2, 3):
        back_arrived(kind)

    @pl.loop(1, RING)
    def _(s):
        at = (z + s) % RING

        @pl.when(owns(at, idle))
        def _():
            for kind in range(5):
                send(kind, at).wait_send()

        @pl.when(mine)
        def _():
            for kind in range(4):
                back(kind, at).wait_send()

        z_sum(s).wait_send()
        z_all(s).wait_send()

    @pl.when(mine)
    def _():
        @pl.loop(0, RING)
        def _(at):
            for kind in (0, 1):
                hop(kind, at, False)

        for kind in (0, 1):
            @pl.when(has_down)
            def _():
                halo(kind, False).wait_send()

            @pl.when(has_up)
            def _():
                halo(kind, True).wait_send()

    for c in (cot_y, cot_core, cot_on, y2_send, y1_send, to_core, to_y, all_1y, all_2y):
        c.wait_send()
    for c in (first, second, spread_1, spread_2):
        c.sent()


def step(listed, tokens, q, k, v, cot, w):
    any_space = pl.BlockSpec(memory_space=pl.ANY)
    vmem = pl.BlockSpec(memory_space=pltpu.VMEM)
    smem = pl.BlockSpec(memory_space=pltpu.SMEM)
    dma = pltpu.SemaphoreType.DMA
    grad = jax.ShapeDtypeStruct((TILE, FEAT), BF16)

    def tiles(n, dtype=BF16):
        return pltpu.VMEM((n, TILE, HEAD_DIM), dtype)

    return pl.pallas_call(
        step_kernel,
        out_shape=(
            jax.ShapeDtypeStruct((TILE, DBLK), BF16), grad, grad, grad,
            jax.ShapeDtypeStruct((FEAT, DOUT), BF16),
        ),
        in_specs=[smem, smem, any_space, any_space, any_space, vmem, vmem],
        out_specs=(vmem, any_space, any_space, any_space, any_space),
        scratch_shapes=[
            pltpu.VMEM((8, 128), jnp.int32),
            pltpu.VMEM((RING, 8, 128), jnp.int32),
            pltpu.SMEM((RING, 8, 128), jnp.int32),
            tiles(2 * RING),
            tiles(2 * RING),
            tiles(RING),
            tiles(RING),
            pltpu.VMEM((GRP, TILE, DBLK), BF16),
            tiles(HEADS),
            pltpu.VMEM((KEYS, TILE), F32),
            pltpu.VMEM((RING, KEYS, TILE), BF16),
            pltpu.VMEM((KEYS, HEAD_DIM), BF16),
            tiles(NB + 1, F32),
            pltpu.VMEM((RING, HEAD_DIM, TILE), F32),
            tiles(2 * RING + 2, F32),
            tiles(2 * RING + 2, F32),
            tiles(RING),
            tiles(RING),
            pltpu.VMEM((TILE, FEAT), BF16),
            tiles(RING),
            tiles(RING),
            tiles(RING),
            tiles(RING),
            tiles(RING),
            tiles(RING),
            pltpu.VMEM((FEAT, DOUT), BF16),
            pltpu.VMEM((6, XROWS, QUARTER), BF16),
            pltpu.VMEM((6, SROWS, QUARTER), BF16),
            pltpu.VMEM((2, XROWS, QUARTER), BF16),
            pltpu.VMEM((2, SROWS, QUARTER), BF16),
            pltpu.VMEM((2, XROWS, QUARTER), F32),
            pltpu.VMEM((SROWS, HALF), BF16),
            pltpu.VMEM((SROWS, HALF), BF16),
            pltpu.VMEM((YROWS, HALF), BF16),
            pltpu.VMEM((YROWS, HALF), BF16),
            pltpu.VMEM((SROWS, DOUT), BF16),
            pltpu.VMEM((RING, ZROWS, ZCOLS), BF16),
            pltpu.VMEM((ZROWS, ZCOLS), BF16),
            pltpu.VMEM((2, TILE, DBLK), F32),
            pltpu.VMEM((2, TILE, DBLK), F32),
            pltpu.VMEM((2, TILE, DBLK), F32),
            pltpu.VMEM((TILE, DBLK), BF16),
            pltpu.VMEM((TILE, DBLK), BF16),
            dma((5, RING)),
            dma((5, RING)),
            dma((6,)),
            dma((3,)),
            dma((3,)),
            dma((1,)),
            dma((2, RING)),
            dma((2, RING)),
            dma((4, RING)),
            dma((4, HEADS)),
            dma((5,)),
            dma((2, 2)),
            dma((2, 2)),
            dma((24,)),
            dma((24,)),
            dma((4,)),
            dma((4,)),
            dma((2, RING)),
            dma((2, RING)),
            dma((2,)),
            dma((2,)),
        ],
        compiler_params=pltpu.CompilerParams(
            collective_id=0, has_side_effects=True, vmem_limit_bytes=VMEM_LIMIT
        ),
        name="step",
    )(listed, tokens, q, k, v, cot, w)


def settle_kernel(*refs):
    count = len(refs) // 2
    sems = refs[-1]
    copies = []
    for n in range(count):
        src, dst = refs[n], refs[count + n]
        rows = src.shape[0] // 4
        for part in range(4):
            here = pl.ds(part * rows, rows)
            copies.append(pltpu.make_async_copy(src.at[here], dst.at[here], sems.at[n, part]))
    for c in copies:
        c.start()
    for c in copies:
        c.wait()


def settle(arrays):
    any_space = pl.BlockSpec(memory_space=pl.ANY)
    return pl.pallas_call(
        settle_kernel,
        out_shape=tuple(jax.ShapeDtypeStruct(a.shape, a.dtype) for a in arrays),
        in_specs=[any_space] * len(arrays),
        out_specs=(any_space,) * len(arrays),
        scratch_shapes=[pltpu.SemaphoreType.DMA((len(arrays), 4))],
        name="settle",
    )(*arrays)


def body(query_tokens, key_tokens, value_tokens, w_out, cotangent, neighbours, tile_tokens):
    return settle(
        step(neighbours, tile_tokens, query_tokens, key_tokens, value_tokens, cotangent, w_out)
    )


def solution(mesh):
    placed = (
        P("tile", "grp"),
        P("tile", "grp"),
        P("tile", "grp"),
        P("grp", None),
        P("tile", "grp"),
        P("tile", None),
        P(),
    )
    return jax.shard_map(
        body,
        mesh=mesh,
        in_specs=placed,
        out_specs=(
            P("tile", "grp"),
            P("tile", "grp"),
            P("tile", "grp"),
            P("tile", "grp"),
            P("grp", None),
        ),
        check_vma=False,
    )
```

```python
import math

import jax
import jax.numpy as jnp
from jax import lax
from jax.experimental import pallas as pl
from jax.experimental.pallas import tpu as pltpu
from jax.sharding import PartitionSpec as P

MESH = pl.DeviceIdType.MESH
HEAD_DIM = 128
TILE = 384
NB = 5
HEADS = 6
RING = 8
RINGS = 8
FEAT = HEADS * HEAD_DIM
GRP = 4
DBLK = 384
DOUT = GRP * DBLK
FACTOR = 1.0 / math.sqrt(HEAD_DIM)
BF16 = jnp.bfloat16
F32 = jnp.float32
VMEM_LIMIT = 56 * 1024 * 1024


def whereabouts():
    tile = lax.axis_index("tile")
    grp = lax.axis_index("grp")
    z = tile % RING
    ring = tile // RING
    core = grp % 2
    idle = 3 - 2 * core
    return tile, grp, z, ring, core, idle


def owns(z, idle):
    return z % 4 != idle


def head_at(z, idle):
    zz = z % 4
    return (z // 4) * 3 + zz - jnp.where(zz > idle, 1, 0)


def place_of(head, idle):
    hh = head % 3
    return (head // 3) * 4 + hh + jnp.where(hh >= idle, 1, 0)


def head_cols(head):
    return pl.ds(pl.multiple_of(head * HEAD_DIM, HEAD_DIM), HEAD_DIM)


def remote(src, dst, send_sem, recv_sem, **where):
    return pltpu.make_async_remote_copy(
        src_ref=src,
        dst_ref=dst,
        send_sem=send_sem,
        recv_sem=recv_sem,
        device_id=where,
        device_id_type=MESH,
    )


def signal(barrier, **where):
    pl.semaphore_signal(barrier, inc=1, device_id=where, device_id_type=MESH)


def greet_ring(barrier, tile, z, ring):
    @pl.loop(1, RING)
    def _(s):
        signal(barrier, tile=tile - z + (z + s) % RING)

    @pl.when(ring > 0)
    def _():
        signal(barrier, tile=tile - RING)

    @pl.when(ring < RINGS - 1)
    def _():
        signal(barrier, tile=tile + RING)


def ring_edges(ring):
    return jnp.where(ring > 0, 1, 0) + jnp.where(ring < RINGS - 1, 1, 0)

XROWS = FEAT // 4
YROWS = FEAT // 2
SROWS = FEAT // 8
ZROWS = SROWS // 2
ZCOLS = DOUT // 4
HALF = DOUT // 2
QUARTER = DOUT // 4
KEYS = NB * TILE
SHIFTS = tuple((dt, dh) for dt in (-1, 0, 1) for dh in (-1, 0, 1) if (dt, dh) != (0, 0))
LOG2E = math.log2(math.e)


def nt(a, b):
    return lax.dot_general(a, b, (((1,), (1,)), ((), ())), preferred_element_type=F32)


def tn(a, b):
    return lax.dot_general(a, b, (((0,), (0,)), ((), ())), preferred_element_type=F32)


def step_kernel(
    listed, tokens, q, k, v, cot, w,
    bo, dq, dk, dv, dw,
    nb_o, nb_v, nb_s, k16, v16, q8, g8, cot_s, g_loc, s_scr, p, vc, tmp, o_t, acck, accv,
    att8, dq8, att_s, hk, hv, hks, hvs, dkb, dvb,
    dwp, x1, x2, xs1, xs2, x_tot, y1s, y1l, y2l, y2, zs, zl, fin, pos, pol, own, ybs, ybl,
    ssem, rsem, lsem, csend, crecv, clocal, khsend, khrecv, osend, orecv, olocal, hsend, hrecv,
    xsend, xrecv, ysend, yrecv, zsend, zrecv, gsend, grecv,
):
    tile, grp, z, ring, core, idle = whereabouts()
    base = tile - z
    mine = owns(z, idle)
    my_head = head_at(z, idle)
    x = ring % 4
    y = ring // 4
    right = tile - x * RING + (x + 1) % 4 * RING
    left = tile - x * RING + (x + 3) % 4 * RING
    y_pair = tile + 32 - 64 * y
    other_core = grp + 1 - 2 * core
    other_y = (grp + 2) % GRP
    y_hi = grp // 2
    has_up = ring < RINGS - 1
    has_down = ring > 0

    barrier = pltpu.get_barrier_semaphore()
    greet_ring(barrier, tile, z, ring)
    for where in (right, left, y_pair):
        signal(barrier, tile=where)
    signal(barrier, grp=other_core)
    signal(barrier, grp=other_y)
    pl.semaphore_wait(barrier, RING - 1 + 5 + ring_edges(ring))

    cot_y = remote(cot, cot_s.at[grp], csend.at[0], crecv.at[0], grp=other_y)
    cot_core = remote(cot, cot_s.at[grp], csend.at[1], crecv.at[1], grp=other_core)
    cot_y.start()
    cot_core.start()
    cot_own = pltpu.make_async_copy(cot, cot_s.at[grp], clocal.at[0])
    cot_own.start()

    def ends(kind, at):
        cols = head_cols(head_at(at, idle))
        if kind == 0:
            return k.at[:, cols], k16.at[z + 4]
        if kind == 1:
            return v.at[:, cols], v16.at[z + 4]
        if kind == 2:
            return q.at[:, cols], q8.at[z]
        if kind == 3:
            return g_loc.at[head_at(at, idle)], g8.at[z]
        return nb_o, nb_v.at[z]

    def send(kind, at):
        src, dst = ends(kind, at)
        return remote(src, dst, ssem.at[kind, at], rsem.at[kind, z], tile=base + at)

    def keep(kind):
        src, dst = ends(kind, z)
        return pltpu.make_async_copy(src, dst, lsem.at[kind])

    def arrived(kind, at):
        dst = (k16.at[at + 4], v16.at[at + 4], q8.at[at], g8.at[at], nb_v.at[at])[kind]
        return remote(dst, dst, ssem.at[kind, 0], rsem.at[kind, at], tile=base + at)

    def send_kinds(kinds):
        @pl.loop(1, RING)
        def _(s):
            at = (z + s) % RING

            @pl.when(owns(at, idle))
            def _():
                for kind in kinds:
                    send(kind, at).start()

        @pl.when(mine)
        def _():
            for kind in kinds:
                keep(kind).start()

    down = lax.broadcasted_iota(jnp.int32, (8, 128), 0)
    across = lax.broadcasted_iota(jnp.int32, (8, 128), 1)
    table = jnp.zeros((8, 128), jnp.int32)
    ids = [listed[0, j] for j in range(NB)]
    for j, n in enumerate(ids):
        near = jnp.where(n >= 0, n - ring * RING + 4, z + 4)
        near = jnp.clip(near, 0, 2 * RING - 1)
        table = jnp.where((down == 0) & (across == j), near, table)
        alive = jnp.where(n >= 0, tokens[jnp.maximum(n, 0)], 0)
        table = jnp.where((down == 1) & (across == j), alive, table)
    for c, (dt, dh) in enumerate(SHIFTS):
        slot = jnp.int32(NB)
        for j in range(1, NB):
            hit = (ids[j] >= 0) & (ids[j] == tile + dt * 4 + dh)
            slot = slot - jnp.where(hit, NB - j, 0)
        table = jnp.where((down == 2) & (across == c), jnp.maximum(slot, 0), table)
    nb_o[...] = table

    send_kinds((4, 0))
    send_kinds((2,))

    remote(cot, cot_s.at[other_y], csend.at[0], crecv.at[0], grp=other_y).wait_recv()
    cot_on = remote(cot_s.at[other_y], cot_s.at[other_y], csend.at[2], crecv.at[2], grp=other_core)
    cot_on.start()
    far = (other_core + 2) % GRP
    remote(cot, cot_s.at[other_core], csend.at[1], crecv.at[1], grp=other_core).wait_recv()
    remote(cot, cot_s.at[far], csend.at[2], crecv.at[2], grp=other_core).wait_recv()
    cot_own.wait()

    @pl.loop(0, HEADS)
    def _(h):
        total = None
        for b in range(GRP):
            part = nt(cot_s[b], w[head_cols(h), b * DBLK:(b + 1) * DBLK])
            total = part if total is None else total + part
        g_loc[h] = total.astype(BF16)

    send_kinds((1,))

    def hop(kind, at, start):
        buf = (k16, v16)[kind]

        def go(c):
            if start:
                c.start()
            else:
                c.wait_send()

        @pl.when((at >= 4) & has_up)
        def _():
            go(remote(buf.at[at + 4], buf.at[at - 4], khsend.at[kind, at], khrecv.at[kind, at],
                      tile=tile + RING))

        @pl.when((at < 4) & has_down)
        def _():
            go(remote(buf.at[at + 4], buf.at[at + 12], khsend.at[kind, at], khrecv.at[kind, at],
                      tile=tile - RING))

    def hops_arrived(kind):
        buf = (k16, v16)[kind]

        @pl.loop(0, RING)
        def _(at):
            @pl.when((at >= 4) & has_down)
            def _():
                remote(buf.at[at - 4], buf.at[at - 4], khsend.at[kind, at], khrecv.at[kind, at],
                       tile=tile - RING).wait_recv()

            @pl.when((at < 4) & has_up)
            def _():
                remote(buf.at[at + 12], buf.at[at + 12], khsend.at[kind, at], khrecv.at[kind, at],
                       tile=tile + RING).wait_recv()

    def back_ends(kind, at, h):
        src = (att8, dq8, dkb, dvb)[kind].at[at]
        dst = (att_s, dq, dk, dv)[kind].at[:, head_cols(h)]
        return src, dst

    def back(kind, at):
        src, dst = back_ends(kind, at, my_head)
        return remote(src, dst, osend.at[kind, at], orecv.at[kind, my_head], tile=base + at)

    def back_own(kind):
        src, dst = back_ends(kind, z, my_head)
        return pltpu.make_async_copy(src, dst, olocal.at[kind])

    def back_start(kind, at):
        @pl.when(at != z)
        def _():
            back(kind, at).start()

        @pl.when(at == z)
        def _():
            back_own(kind).start()

    def back_arrived(kind):
        @pl.loop(0, HEADS)
        def _(h):
            at = place_of(h, idle)
            src, dst = back_ends(kind, z, h)

            @pl.when(at != z)
            def _():
                remote(src, dst, osend.at[kind, 0], orecv.at[kind, h], tile=base + at).wait_recv()

        @pl.when(mine)
        def _():
            back_own(kind).wait()

    def local(r, j):
        return nb_s[r, 0, j]

    def count(r, j):
        return nb_s[r, 1, j]

    def gather(acc, r):
        acc[r + 5] += tmp[0]
        for n, (dt, dh) in enumerate(SHIFTS):
            acc[r + 5 + dt * 4 + dh] += tmp[nb_s[r, 2, n]]

    def weigh(r):
        queries = q8[r]
        rows = lax.broadcasted_iota(jnp.int32, (TILE, TILE), 0)
        top = jnp.full((8, TILE), -1e30, F32)
        for j in range(NB):
            s = nt(k16[local(r, j)], queries)
            s = jnp.where(rows < count(r, j), s, F32(-1e30))
            s_scr[j * TILE:(j + 1) * TILE, :] = s
            top = jnp.maximum(top, jnp.max(s.reshape(TILE // 8, 8, TILE), axis=0))
        top = jnp.max(top, axis=0, keepdims=True)
        total = jnp.zeros((8, TILE), F32)
        for j in range(NB):
            e = jnp.exp2((s_scr[j * TILE:(j + 1) * TILE, :] - top) * F32(FACTOR * LOG2E))
            s_scr[j * TILE:(j + 1) * TILE, :] = e
            total = total + jnp.sum(e.reshape(TILE // 8, 8, TILE), axis=0)
        inverse = 1.0 / jnp.sum(total, axis=0, keepdims=True)
        for j in range(NB):
            p[r, j * TILE:(j + 1) * TILE, :] = (
                s_scr[j * TILE:(j + 1) * TILE, :] * inverse
            ).astype(BF16)

    def attend(r):
        for j in range(NB):
            vc[j * TILE:(j + 1) * TILE, :] = v16[local(r, j)]
        out = tn(vc[...], p[r])
        o_t[r] = out
        att8[r] = out.T.astype(BF16)

    def value_part(r):
        tmp[0:NB] = jnp.dot(p[r], g8[r], preferred_element_type=F32).reshape(NB, TILE, HEAD_DIM)
        gather(accv, r)

    def key_part(r):
        grads = g8[r]
        delta = jnp.sum(o_t[r] * grads.astype(F32).T, axis=0, keepdims=True)
        for j in range(NB):
            rows = slice(j * TILE, (j + 1) * TILE)
            gp = nt(v16[local(r, j)], grads)
            ds = p[r, rows, :].astype(F32) * ((gp - delta) * F32(FACTOR))
            p[r, rows, :] = ds.astype(BF16)
        keys = jnp.dot(p[r], q8[r], preferred_element_type=F32)
        tmp[0:NB] = keys.reshape(NB, TILE, HEAD_DIM)
        gather(acck, r)

    def query_part(r):
        for j in range(NB):
            vc[j * TILE:(j + 1) * TILE, :] = k16[local(r, j)]
        dq8[r] = tn(vc[...], p[r]).T.astype(BF16)

    def halo(kind, up):
        src, dst = ((hks, hk), (hvs, hv))[kind]
        if up:
            return remote(src.at[pl.ds(4, 4)], dst.at[pl.ds(0, 4)], hsend.at[kind, 1],
                          hrecv.at[kind, 0], tile=tile + RING)
        return remote(src.at[pl.ds(0, 4)], dst.at[pl.ds(4, 4)], hsend.at[kind, 0],
                      hrecv.at[kind, 1], tile=tile - RING)

    def halo_start(kind):
        acc, src = ((acck, hks), (accv, hvs))[kind]

        @pl.when(has_down)
        def _():
            @pl.loop(0, 4)
            def _(i):
                src[i] = acc[i + 1].astype(BF16)
            halo(kind, False).start()

        @pl.when(has_up)
        def _():
            @pl.loop(0, 4)
            def _(i):
                src[i + 4] = acc[i + 13].astype(BF16)
            halo(kind, True).start()

    def home(kind):
        acc, got, out = ((acck, hk, dkb), (accv, hv, dvb))[kind]

        @pl.when(has_down)
        def _():
            halo(kind, True).wait_recv()

        @pl.when(has_up)
        def _():
            halo(kind, False).wait_recv()

        @pl.loop(0, RING)
        def _(s):
            at = (z + s) % RING
            given = ((at < 4) & has_down) | ((at >= 4) & has_up)

            @pl.when(given)
            def _():
                out[at] = (acc[at + 5] + got[at].astype(F32)).astype(BF16)

            @pl.when(jnp.logical_not(given))
            def _():
                out[at] = acc[at + 5].astype(BF16)

            back_start(2 + kind, at)

    def blk(i, size):
        return pl.ds(pl.multiple_of(i % 4 * size, size), size)

    class Line:
        def __init__(self, src, first, size, land, stage, slot):
            a, b = pl.ds(first, QUARTER), pl.ds(first + QUARTER, QUARTER)
            self.src, self.cols, self.size, self.land, self.stage = src, (a, b), size, land, stage

            def leg(i, col, n, to):
                return remote(src.at[blk(i, size), col], land.at[n], xsend.at[slot + n],
                              xrecv.at[slot + n], tile=to)

            self.rel = (leg(x + 2, a, 0, left), leg(x + 2, b, 1, right))
            self.one = (leg(x + 1, a, 2, right), leg(x + 3, b, 3, left))
            self.sum = tuple(
                remote(stage.at[n], land.at[4 + n], xsend.at[slot + 4 + n], xrecv.at[slot + 4 + n],
                       tile=(left, right)[n])
                for n in range(2)
            )

        def start(self):
            for c in self.rel + self.one:
                c.start()

        def relay(self):
            for n in range(2):
                self.rel[n].wait_recv()
                mine_too = self.src[blk(x + (3, 1)[n], self.size), self.cols[n]]
                self.stage[n] = (self.land[n].astype(F32) + mine_too.astype(F32)).astype(BF16)
                self.sum[n].start()

        def total(self, n):
            self.one[n].wait_recv()
            self.sum[n].wait_recv()
            here = self.src[blk(x, self.size), self.cols[n]]
            return here.astype(F32) + self.land[2 + n].astype(F32) + self.land[4 + n].astype(F32)

        def sent(self):
            for c in self.rel + self.one + self.sum:
                c.wait_send()

    first = Line(dwp, 0, XROWS, x1, xs1, 0)
    second = Line(y2, 0, SROWS, x2, xs2, 6)

    def half_rows(i):
        return pl.ds(pl.multiple_of(i * YROWS, YROWS), YROWS)

    y2_send = remote(dwp.at[half_rows(1 - y), pl.ds(HALF, HALF)], y2l, ysend.at[0], yrecv.at[0],
                     tile=y_pair)
    y1_send = remote(y1s, y1l, ysend.at[1], yrecv.at[1], tile=y_pair)
    to_core = remote(pos, pol, gsend.at[0], grecv.at[0], grp=other_core)
    to_y = remote(ybs, ybl, gsend.at[1], grecv.at[1], grp=other_y)

    def projected(b):
        cols = pl.ds(pl.multiple_of(b * DBLK, DBLK), DBLK)
        return jnp.dot(att_s[...], w[:, cols], preferred_element_type=F32)

    def stage_1():
        back_arrived(0)

        def part(first_head, count, blocks):
            @pl.loop(first_head, first_head + count)
            def _(h):
                rows = head_cols(h)
                turned = att_s[:, rows].T
                for b in blocks:
                    dwp[rows, b * DBLK:(b + 1) * DBLK] = jnp.dot(
                        turned, cot_s[b], preferred_element_type=F32
                    ).astype(BF16)

        per_half = HEADS // 2
        part((1 - y) * per_half, per_half, (2, 3))
        y2_send.start()
        part(0, HEADS, (0, 1))
        first.start()
        part(y * per_half, per_half, (2, 3))

        @pl.loop(0, 2)
        def _(yy):
            pos[yy] = projected(yy * 2 + 1 - core)

        to_core.start()

        @pl.loop(0, 2)
        def _(yy):
            own[yy] = projected(yy * 2 + core)

    def stage_2():
        first.relay()

    def stage_3():
        y2_send.wait_recv()
        y2[...] = (
            dwp[half_rows(y), HALF:].astype(F32) + y2l[...].astype(F32)
        ).astype(BF16)
        second.start()
        to_core.wait_recv()
        ybs[...] = (own[1 - y_hi] + pol[1 - y_hi]).astype(BF16)
        to_y.start()

    def mid_rows(i):
        return pl.ds(pl.multiple_of(i * SROWS, SROWS), SROWS)

    def stage_4():
        for n in range(2):
            cols = slice(n * QUARTER, (n + 1) * QUARTER)
            total = first.total(n)
            x_tot[n] = total
            y1s[:, cols] = x_tot[n, mid_rows(1 - y), :].astype(BF16)
        y1_send.start()
        second.relay()

    def stage_5():
        for n in range(2):
            zs[:, HALF + n * QUARTER:HALF + (n + 1) * QUARTER] = second.total(n).astype(BF16)
        y1_send.wait_recv()
        for n in range(2):
            cols = slice(n * QUARTER, (n + 1) * QUARTER)
            zs[:, cols] = (x_tot[n, mid_rows(y), :] + y1l[:, cols].astype(F32)).astype(BF16)

        @pl.loop(1, RING)
        def _(s):
            z_sum(s).start()

    def zpart(at):
        return (
            pl.ds(pl.multiple_of(at // 4 * ZROWS, ZROWS), ZROWS),
            pl.ds(pl.multiple_of(at % 4 * ZCOLS, ZCOLS), ZCOLS),
        )

    def z_sum(s):
        at = (z + s) % RING
        return remote(zs.at[zpart(at)], zl.at[z], zsend.at[0, s], zrecv.at[0, z], tile=base + at)

    def finished(at):
        row = jnp.where(at % 4 < 2, x * XROWS + y * SROWS, y * YROWS + x * SROWS)
        rows = pl.ds(pl.multiple_of(row + at // 4 * ZROWS, ZROWS), ZROWS)
        return dw.at[rows, zpart(at)[1]]

    def z_all(s):
        at = (z + s) % RING
        return remote(fin, finished(z), zsend.at[1, s], zrecv.at[1, z], tile=base + at)

    fin_own = pltpu.make_async_copy(fin, finished(z), olocal.at[4])

    def stage_6():
        rows, cols = zpart(z)
        total = zs[rows, cols].astype(F32)
        for s in range(1, RING):
            at = (z + s) % RING
            remote(zl.at[at], zl.at[at], zsend.at[0, 0], zrecv.at[0, at], tile=base + at).wait_recv()
            total += zl[at].astype(F32)
        fin[...] = total.astype(BF16)

        @pl.loop(1, RING)
        def _(s):
            z_all(s).start()

        fin_own.start()

    lo, hi = pl.ds(0, HALF), pl.ds(HALF, HALF)

    def slab_1y(yy):
        return dw.at[pl.ds(pl.multiple_of(x * XROWS + yy * SROWS, SROWS), SROWS), lo]

    def slab_2y(yy):
        return dw.at[half_rows(yy), hi]

    all_1y = remote(slab_1y(y), slab_1y(y), ysend.at[2], yrecv.at[2], tile=y_pair)
    got_1y = remote(slab_1y(1 - y), slab_1y(1 - y), ysend.at[2], yrecv.at[2], tile=y_pair)
    all_2y = remote(slab_2y(y), slab_2y(y), ysend.at[3], yrecv.at[3], tile=y_pair)
    got_2y = remote(slab_2y(1 - y), slab_2y(1 - y), ysend.at[3], yrecv.at[3], tile=y_pair)

    class Spread:
        def __init__(self, rows, cols, slot):
            def part(i, n, k, to):
                ref = dw.at[rows(i), pl.ds(cols + n * QUARTER, QUARTER)]
                return remote(ref, ref, xsend.at[slot + k], xrecv.at[slot + k], tile=to)

            self.outs = (
                part(x, 0, 0, right), part(x, 1, 1, left), part(x, 1, 2, right), part(x, 0, 3, left)
            )
            self.near = (part(x + 3, 0, 0, left), part(x + 1, 1, 1, right))
            self.on = (part(x + 3, 0, 4, right), part(x + 1, 1, 5, left))
            self.rest = (
                part(x + 3, 1, 2, left), part(x + 1, 0, 3, right),
                part(x + 2, 0, 4, left), part(x + 2, 1, 5, right),
            )

        def start(self):
            for c in self.outs:
                c.start()

        def relay(self):
            for n in range(2):
                self.near[n].wait_recv()
                self.on[n].start()

        def finish(self):
            for c in self.rest:
                c.wait_recv()

        def sent(self):
            for c in self.outs + self.on:
                c.wait_send()

    spread_1 = Spread(lambda i: blk(i, XROWS), 0, 12)
    spread_2 = Spread(
        lambda i: pl.ds(pl.multiple_of(y * YROWS + i % 4 * SROWS, SROWS), SROWS), HALF, 18
    )

    def stage_7():
        @pl.loop(1, RING)
        def _(s):
            at = (z + s) % RING
            remote(fin, finished(at), zsend.at[1, 0], zrecv.at[1, at], tile=base + at).wait_recv()

        fin_own.wait()
        spread_2.start()
        all_1y.start()

    def stage_8():
        spread_2.relay()
        got_1y.wait_recv()
        spread_1.start()
        to_y.wait_recv()
        bo[...] = (own[y_hi] + pol[y_hi] + ybl[...].astype(F32)).astype(BF16)

    def stage_9():
        spread_2.finish()
        all_2y.start()
        spread_1.relay()

    def stage_10():
        got_2y.wait_recv()
        spread_1.finish()

    @pl.when(mine)
    def _():
        acck[...] = jnp.zeros_like(acck)
        accv[...] = jnp.zeros_like(accv)
        tmp[NB] = jnp.zeros((TILE, HEAD_DIM), F32)
        keep(0).wait()
        hop(0, z, True)

        @pl.loop(1, RING)
        def _(s):
            at = (z + RING - s) % RING
            arrived(0, at).wait_recv()
            hop(0, at, True)

        keep(4).wait()

        @pl.loop(1, RING)
        def _(s):
            arrived(4, (z + RING - s) % RING).wait_recv()

        lists = pltpu.make_async_copy(nb_v, nb_s, lsem.at[5])
        lists.start()
        hops_arrived(0)
        lists.wait()

        def ready(kind, i):
            @pl.when(i == 0)
            def _():
                keep(kind).wait()

            @pl.when(i > 0)
            def _():
                arrived(kind, (z + RING - i) % RING).wait_recv()

        @pl.loop(0, RING)
        def _(i):
            ready(2, i)
            weigh((z + RING - i) % RING)

            @pl.when(i >= 4)
            def _():
                for n in range(2):
                    s = (i - 4) * 2 + n
                    ready(1, s)
                    hop(1, (z + RING - s) % RING, True)

        hops_arrived(1)

        @pl.loop(0, RING)
        def _(i):
            r = (z + RING - i) % RING
            attend(r)
            back_start(0, r)

    @pl.when(jnp.logical_not(mine))
    def _():
        @pl.loop(1, RING)
        def _(s):
            at = (z + s) % RING

            @pl.when(owns(at, idle))
            def _():
                send(1, at).wait_send()

    send_kinds((3,))
    stage_1()

    def steps(work, stages):
        @pl.loop(0, RING)
        def _(i):
            pl.when(mine)(lambda: work(i))
            for n, stage in stages:
                pl.when(i == n)(stage)

    def owner(stage):
        return lambda: pl.when(mine)(stage)

    def value_step(i):
        @pl.when(i == 0)
        def _():
            keep(3).wait()

        @pl.when(i > 0)
        def _():
            arrived(3, (z + RING - i) % RING).wait_recv()

        value_part((z + RING - i) % RING)

    def query_step(i):
        r = (z + i) % RING
        query_part(r)
        back_start(1, r)

    steps(value_step, ((5, stage_2), (7, owner(lambda: halo_start(1)))))
    steps(
        lambda i: key_part((z + i) % RING),
        (
            (1, stage_3), (3, stage_4), (4, stage_5), (4, owner(lambda: home(1))), (6, stage_6),
            (7, owner(lambda: halo_start(0))),
        ),
    )
    steps(
        query_step,
        ((1, stage_7), (3, stage_8), (4, owner(lambda: home(0))), (6, stage_9)),
    )
    stage_10()

    for kind in (1, 2, 3):
        back_arrived(kind)

    @pl.loop(1, RING)
    def _(s):
        at = (z + s) % RING

        @pl.when(owns(at, idle))
        def _():
            for kind in (0, 2, 3, 4):
                send(kind, at).wait_send()

            @pl.when(mine)
            def _():
                send(1, at).wait_send()

        @pl.when(mine)
        def _():
            for kind in range(4):
                back(kind, at).wait_send()

        z_sum(s).wait_send()
        z_all(s).wait_send()

    @pl.when(mine)
    def _():
        @pl.loop(0, RING)
        def _(at):
            for kind in (0, 1):
                hop(kind, at, False)

        for kind in (0, 1):
            @pl.when(has_down)
            def _():
                halo(kind, False).wait_send()

            @pl.when(has_up)
            def _():
                halo(kind, True).wait_send()

    for c in (cot_y, cot_core, cot_on, y2_send, y1_send, to_core, to_y, all_1y, all_2y):
        c.wait_send()
    for c in (first, second, spread_1, spread_2):
        c.sent()


def step(listed, tokens, q, k, v, cot, w):
    any_space = pl.BlockSpec(memory_space=pl.ANY)
    vmem = pl.BlockSpec(memory_space=pltpu.VMEM)
    smem = pl.BlockSpec(memory_space=pltpu.SMEM)
    dma = pltpu.SemaphoreType.DMA
    grad = jax.ShapeDtypeStruct((TILE, FEAT), BF16)

    def tiles(n, dtype=BF16):
        return pltpu.VMEM((n, TILE, HEAD_DIM), dtype)

    return pl.pallas_call(
        step_kernel,
        out_shape=(
            jax.ShapeDtypeStruct((TILE, DBLK), BF16), grad, grad, grad,
            jax.ShapeDtypeStruct((FEAT, DOUT), BF16),
        ),
        in_specs=[smem, smem, any_space, any_space, any_space, vmem, vmem],
        out_specs=(vmem, any_space, any_space, any_space, any_space),
        scratch_shapes=[
            pltpu.VMEM((8, 128), jnp.int32),
            pltpu.VMEM((RING, 8, 128), jnp.int32),
            pltpu.SMEM((RING, 8, 128), jnp.int32),
            tiles(2 * RING),
            tiles(2 * RING),
            tiles(RING),
            tiles(RING),
            pltpu.VMEM((GRP, TILE, DBLK), BF16),
            tiles(HEADS),
            pltpu.VMEM((KEYS, TILE), F32),
            pltpu.VMEM((RING, KEYS, TILE), BF16),
            pltpu.VMEM((KEYS, HEAD_DIM), BF16),
            tiles(NB + 1, F32),
            pltpu.VMEM((RING, HEAD_DIM, TILE), F32),
            tiles(2 * RING + 2, F32),
            tiles(2 * RING + 2, F32),
            tiles(RING),
            tiles(RING),
            pltpu.VMEM((TILE, FEAT), BF16),
            tiles(RING),
            tiles(RING),
            tiles(RING),
            tiles(RING),
            tiles(RING),
            tiles(RING),
            pltpu.VMEM((FEAT, DOUT), BF16),
            pltpu.VMEM((6, XROWS, QUARTER), BF16),
            pltpu.VMEM((6, SROWS, QUARTER), BF16),
            pltpu.VMEM((2, XROWS, QUARTER), BF16),
            pltpu.VMEM((2, SROWS, QUARTER), BF16),
            pltpu.VMEM((2, XROWS, QUARTER), F32),
            pltpu.VMEM((SROWS, HALF), BF16),
            pltpu.VMEM((SROWS, HALF), BF16),
            pltpu.VMEM((YROWS, HALF), BF16),
            pltpu.VMEM((YROWS, HALF), BF16),
            pltpu.VMEM((SROWS, DOUT), BF16),
            pltpu.VMEM((RING, ZROWS, ZCOLS), BF16),
            pltpu.VMEM((ZROWS, ZCOLS), BF16),
            pltpu.VMEM((2, TILE, DBLK), F32),
            pltpu.VMEM((2, TILE, DBLK), F32),
            pltpu.VMEM((2, TILE, DBLK), F32),
            pltpu.VMEM((TILE, DBLK), BF16),
            pltpu.VMEM((TILE, DBLK), BF16),
            dma((5, RING)),
            dma((5, RING)),
            dma((6,)),
            dma((3,)),
            dma((3,)),
            dma((1,)),
            dma((2, RING)),
            dma((2, RING)),
            dma((4, RING)),
            dma((4, HEADS)),
            dma((5,)),
            dma((2, 2)),
            dma((2, 2)),
            dma((24,)),
            dma((24,)),
            dma((4,)),
            dma((4,)),
            dma((2, RING)),
            dma((2, RING)),
            dma((2,)),
            dma((2,)),
        ],
        compiler_params=pltpu.CompilerParams(
            collective_id=0, has_side_effects=True, vmem_limit_bytes=VMEM_LIMIT
        ),
        name="step",
    )(listed, tokens, q, k, v, cot, w)


def settle_kernel(*refs):
    count = (len(refs) - 1) // 3
    sems = refs[-1]

    def moves(n, part, leg):
        src, dst, held = refs[n], refs[count + n], refs[2 * count + n]
        rows = src.shape[0] // 4
        here = pl.ds(part * rows, rows)
        if leg == 0:
            return pltpu.make_async_copy(src.at[here], held.at[here], sems.at[0, n, part])
        return pltpu.make_async_copy(held.at[here], dst.at[here], sems.at[1, n, part])

    every = [(n, part) for n in range(count) for part in range(4)]
    for n, part in every:
        moves(n, part, 0).start()
    for n, part in every:
        moves(n, part, 0).wait()
        moves(n, part, 1).start()
    for n, part in every:
        moves(n, part, 1).wait()


def settle(arrays):
    any_space = pl.BlockSpec(memory_space=pl.ANY)
    return pl.pallas_call(
        settle_kernel,
        out_shape=tuple(jax.ShapeDtypeStruct(a.shape, a.dtype) for a in arrays),
        in_specs=[any_space] * len(arrays),
        out_specs=(any_space,) * len(arrays),
        scratch_shapes=[pltpu.VMEM(a.shape, a.dtype) for a in arrays]
        + [pltpu.SemaphoreType.DMA((2, len(arrays), 4))],
        compiler_params=pltpu.CompilerParams(vmem_limit_bytes=VMEM_LIMIT),
        name="settle",
    )(*arrays)


def body(query_tokens, key_tokens, value_tokens, w_out, cotangent, neighbours, tile_tokens):
    return settle(
        step(neighbours, tile_tokens, query_tokens, key_tokens, value_tokens, cotangent, w_out)
    )


def solution(mesh):
    placed = (
        P("tile", "grp"),
        P("tile", "grp"),
        P("tile", "grp"),
        P("grp", None),
        P("tile", "grp"),
        P("tile", None),
        P(),
    )
    return jax.shard_map(
        body,
        mesh=mesh,
        in_specs=placed,
        out_specs=(
            P("tile", "grp"),
            P("tile", "grp"),
            P("tile", "grp"),
            P("tile", "grp"),
            P("grp", None),
        ),
        check_vma=False,
    )
```

```python
import math

import jax
import jax.numpy as jnp
from jax import lax
from jax.experimental import pallas as pl
from jax.experimental.pallas import tpu as pltpu
from jax.sharding import PartitionSpec as P

MESH = pl.DeviceIdType.MESH
HEAD_DIM = 128
TILE = 384
NB = 5
HEADS = 6
RING = 8
RINGS = 8
FEAT = HEADS * HEAD_DIM
GRP = 4
DBLK = 384
DOUT = GRP * DBLK
FACTOR = 1.0 / math.sqrt(HEAD_DIM)
BF16 = jnp.bfloat16
F32 = jnp.float32
VMEM_LIMIT = 56 * 1024 * 1024


def whereabouts():
    tile = lax.axis_index("tile")
    grp = lax.axis_index("grp")
    z = tile % RING
    ring = tile // RING
    core = grp % 2
    idle = 3 - 2 * core
    return tile, grp, z, ring, core, idle


def owns(z, idle):
    return z % 4 != idle


def head_at(z, idle):
    zz = z % 4
    return (z // 4) * 3 + zz - jnp.where(zz > idle, 1, 0)


def place_of(head, idle):
    hh = head % 3
    return (head // 3) * 4 + hh + jnp.where(hh >= idle, 1, 0)


def head_cols(head):
    return pl.ds(pl.multiple_of(head * HEAD_DIM, HEAD_DIM), HEAD_DIM)


def remote(src, dst, send_sem, recv_sem, **where):
    return pltpu.make_async_remote_copy(
        src_ref=src,
        dst_ref=dst,
        send_sem=send_sem,
        recv_sem=recv_sem,
        device_id=where,
        device_id_type=MESH,
    )


def signal(barrier, **where):
    pl.semaphore_signal(barrier, inc=1, device_id=where, device_id_type=MESH)


def greet_ring(barrier, tile, z, ring):
    @pl.loop(1, RING)
    def _(s):
        signal(barrier, tile=tile - z + (z + s) % RING)

    @pl.when(ring > 0)
    def _():
        signal(barrier, tile=tile - RING)

    @pl.when(ring < RINGS - 1)
    def _():
        signal(barrier, tile=tile + RING)


def ring_edges(ring):
    return jnp.where(ring > 0, 1, 0) + jnp.where(ring < RINGS - 1, 1, 0)

XROWS = FEAT // 4
YROWS = FEAT // 2
SROWS = FEAT // 8
ZROWS = SROWS // 2
ZCOLS = DOUT // 4
HALF = DOUT // 2
QUARTER = DOUT // 4
KEYS = NB * TILE
SHIFTS = tuple((dt, dh) for dt in (-1, 0, 1) for dh in (-1, 0, 1) if (dt, dh) != (0, 0))
LOG2E = math.log2(math.e)


def nt(a, b):
    return lax.dot_general(a, b, (((1,), (1,)), ((), ())), preferred_element_type=F32)


def tn(a, b):
    return lax.dot_general(a, b, (((0,), (0,)), ((), ())), preferred_element_type=F32)


def step_kernel(
    listed, tokens, q, k, v, cot, w,
    bo, dq, dk, dv, dw,
    nb_o, nb_v, nb_s, k16, v16, q8, g8, cot_s, g_loc, s_scr, p, vc, tmp, o_t, acck, accv,
    att8, dq8, att_s, hk, hv, hks, hvs, dkb, dvb,
    dwp, x1, x2, xs1, xs2, x_tot, y1s, y1l, y2l, y2, zs, zl, fin, pos, pol, own, ybs, ybl,
    ssem, rsem, lsem, csend, crecv, clocal, khsend, khrecv, osend, orecv, olocal, hsend, hrecv,
    xsend, xrecv, ysend, yrecv, zsend, zrecv, gsend, grecv,
):
    tile, grp, z, ring, core, idle = whereabouts()
    base = tile - z
    mine = owns(z, idle)
    my_head = head_at(z, idle)
    x = ring % 4
    y = ring // 4
    right = tile - x * RING + (x + 1) % 4 * RING
    left = tile - x * RING + (x + 3) % 4 * RING
    y_pair = tile + 32 - 64 * y
    other_core = grp + 1 - 2 * core
    other_y = (grp + 2) % GRP
    y_hi = grp // 2
    has_up = ring < RINGS - 1
    has_down = ring > 0

    barrier = pltpu.get_barrier_semaphore()
    greet_ring(barrier, tile, z, ring)
    for where in (right, left, y_pair):
        signal(barrier, tile=where)
    signal(barrier, grp=other_core)
    signal(barrier, grp=other_y)
    pl.semaphore_wait(barrier, RING - 1 + 5 + ring_edges(ring))

    cot_y = remote(cot, cot_s.at[grp], csend.at[0], crecv.at[0], grp=other_y)
    cot_core = remote(cot, cot_s.at[grp], csend.at[1], crecv.at[1], grp=other_core)
    cot_y.start()
    cot_core.start()
    cot_own = pltpu.make_async_copy(cot, cot_s.at[grp], clocal.at[0])
    cot_own.start()

    def ends(kind, at):
        cols = head_cols(head_at(at, idle))
        if kind == 0:
            return k.at[:, cols], k16.at[z + 4]
        if kind == 1:
            return v.at[:, cols], v16.at[z + 4]
        if kind == 2:
            return q.at[:, cols], q8.at[z]
        if kind == 3:
            return g_loc.at[head_at(at, idle)], g8.at[z]
        return nb_o, nb_v.at[z]

    def send(kind, at):
        src, dst = ends(kind, at)
        return remote(src, dst, ssem.at[kind, at], rsem.at[kind, z], tile=base + at)

    def keep(kind):
        src, dst = ends(kind, z)
        return pltpu.make_async_copy(src, dst, lsem.at[kind])

    def arrived(kind, at):
        dst = (k16.at[at + 4], v16.at[at + 4], q8.at[at], g8.at[at], nb_v.at[at])[kind]
        return remote(dst, dst, ssem.at[kind, 0], rsem.at[kind, at], tile=base + at)

    def send_kinds(kinds):
        @pl.loop(1, RING)
        def _(s):
            at = (z + s) % RING

            @pl.when(owns(at, idle))
            def _():
                for kind in kinds:
                    send(kind, at).start()

        @pl.when(mine)
        def _():
            for kind in kinds:
                keep(kind).start()

    down = lax.broadcasted_iota(jnp.int32, (8, 128), 0)
    across = lax.broadcasted_iota(jnp.int32, (8, 128), 1)
    table = jnp.zeros((8, 128), jnp.int32)
    ids = [listed[0, j] for j in range(NB)]
    for j, n in enumerate(ids):
        near = jnp.where(n >= 0, n - ring * RING + 4, z + 4)
        near = jnp.clip(near, 0, 2 * RING - 1)
        table = jnp.where((down == 0) & (across == j), near, table)
        alive = jnp.where(n >= 0, tokens[jnp.maximum(n, 0)], 0)
        table = jnp.where((down == 1) & (across == j), alive, table)
    for c, (dt, dh) in enumerate(SHIFTS):
        slot = jnp.int32(NB)
        for j in range(1, NB):
            hit = (ids[j] >= 0) & (ids[j] == tile + dt * 4 + dh)
            slot = slot - jnp.where(hit, NB - j, 0)
        table = jnp.where((down == 2) & (across == c), jnp.maximum(slot, 0), table)
    nb_o[...] = table

    send_kinds((4, 0))
    send_kinds((2,))

    remote(cot, cot_s.at[other_y], csend.at[0], crecv.at[0], grp=other_y).wait_recv()
    cot_on = remote(cot_s.at[other_y], cot_s.at[other_y], csend.at[2], crecv.at[2], grp=other_core)
    cot_on.start()
    far = (other_core + 2) % GRP
    remote(cot, cot_s.at[other_core], csend.at[1], crecv.at[1], grp=other_core).wait_recv()
    remote(cot, cot_s.at[far], csend.at[2], crecv.at[2], grp=other_core).wait_recv()
    cot_own.wait()

    @pl.loop(0, HEADS)
    def _(h):
        total = None
        for b in range(GRP):
            part = nt(cot_s[b], w[head_cols(h), b * DBLK:(b + 1) * DBLK])
            total = part if total is None else total + part
        g_loc[h] = total.astype(BF16)

    send_kinds((1,))

    def hop(kind, at, start):
        buf = (k16, v16)[kind]

        def go(c):
            if start:
                c.start()
            else:
                c.wait_send()

        @pl.when((at >= 4) & has_up)
        def _():
            go(remote(buf.at[at + 4], buf.at[at - 4], khsend.at[kind, at], khrecv.at[kind, at],
                      tile=tile + RING))

        @pl.when((at < 4) & has_down)
        def _():
            go(remote(buf.at[at + 4], buf.at[at + 12], khsend.at[kind, at], khrecv.at[kind, at],
                      tile=tile - RING))

    def hops_arrived(kind):
        buf = (k16, v16)[kind]

        @pl.loop(0, RING)
        def _(at):
            @pl.when((at >= 4) & has_down)
            def _():
                remote(buf.at[at - 4], buf.at[at - 4], khsend.at[kind, at], khrecv.at[kind, at],
                       tile=tile - RING).wait_recv()

            @pl.when((at < 4) & has_up)
            def _():
                remote(buf.at[at + 12], buf.at[at + 12], khsend.at[kind, at], khrecv.at[kind, at],
                       tile=tile + RING).wait_recv()

    def back_ends(kind, at, h):
        src = (att8, dq8, dkb, dvb)[kind].at[at]
        dst = (att_s, dq, dk, dv)[kind].at[:, head_cols(h)]
        return src, dst

    def back(kind, at):
        src, dst = back_ends(kind, at, my_head)
        return remote(src, dst, osend.at[kind, at], orecv.at[kind, my_head], tile=base + at)

    def back_own(kind):
        src, dst = back_ends(kind, z, my_head)
        return pltpu.make_async_copy(src, dst, olocal.at[kind])

    def back_start(kind, at):
        @pl.when(at != z)
        def _():
            back(kind, at).start()

        @pl.when(at == z)
        def _():
            back_own(kind).start()

    def back_arrived(kind):
        @pl.loop(0, HEADS)
        def _(h):
            at = place_of(h, idle)
            src, dst = back_ends(kind, z, h)

            @pl.when(at != z)
            def _():
                remote(src, dst, osend.at[kind, 0], orecv.at[kind, h], tile=base + at).wait_recv()

        @pl.when(mine)
        def _():
            back_own(kind).wait()

    def local(r, j):
        return nb_s[r, 0, j]

    def count(r, j):
        return nb_s[r, 1, j]

    def gather(acc, r):
        acc[r + 5] += tmp[0]
        for n, (dt, dh) in enumerate(SHIFTS):
            acc[r + 5 + dt * 4 + dh] += tmp[nb_s[r, 2, n]]

    def weigh(r):
        queries = q8[r]
        rows = lax.broadcasted_iota(jnp.int32, (TILE, TILE), 0)
        top = jnp.full((8, TILE), -1e30, F32)
        for j in range(NB):
            s = nt(k16[local(r, j)], queries)
            s = jnp.where(rows < count(r, j), s, F32(-1e30))
            s_scr[j * TILE:(j + 1) * TILE, :] = s
            top = jnp.maximum(top, jnp.max(s.reshape(TILE // 8, 8, TILE), axis=0))
        top = jnp.max(top, axis=0, keepdims=True)
        total = jnp.zeros((8, TILE), F32)
        for j in range(NB):
            e = jnp.exp2((s_scr[j * TILE:(j + 1) * TILE, :] - top) * F32(FACTOR * LOG2E))
            s_scr[j * TILE:(j + 1) * TILE, :] = e
            total = total + jnp.sum(e.reshape(TILE // 8, 8, TILE), axis=0)
        inverse = 1.0 / jnp.sum(total, axis=0, keepdims=True)
        for j in range(NB):
            p[r, j * TILE:(j + 1) * TILE, :] = (
                s_scr[j * TILE:(j + 1) * TILE, :] * inverse
            ).astype(BF16)

    def attend(r):
        for j in range(NB):
            vc[j * TILE:(j + 1) * TILE, :] = v16[local(r, j)]
        out = tn(vc[...], p[r])
        o_t[r] = out
        att8[r] = out.T.astype(BF16)

    def value_part(r):
        tmp[0:NB] = jnp.dot(p[r], g8[r], preferred_element_type=F32).reshape(NB, TILE, HEAD_DIM)
        gather(accv, r)

    def key_part(r):
        grads = g8[r]
        delta = jnp.sum(o_t[r] * grads.astype(F32).T, axis=0, keepdims=True)
        for j in range(NB):
            rows = slice(j * TILE, (j + 1) * TILE)
            gp = nt(v16[local(r, j)], grads)
            ds = p[r, rows, :].astype(F32) * ((gp - delta) * F32(FACTOR))
            p[r, rows, :] = ds.astype(BF16)
        keys = jnp.dot(p[r], q8[r], preferred_element_type=F32)
        tmp[0:NB] = keys.reshape(NB, TILE, HEAD_DIM)
        gather(acck, r)

    def query_part(r):
        for j in range(NB):
            vc[j * TILE:(j + 1) * TILE, :] = k16[local(r, j)]
        dq8[r] = tn(vc[...], p[r]).T.astype(BF16)

    def halo(kind, up):
        src, dst = ((hks, hk), (hvs, hv))[kind]
        if up:
            return remote(src.at[pl.ds(4, 4)], dst.at[pl.ds(0, 4)], hsend.at[kind, 1],
                          hrecv.at[kind, 0], tile=tile + RING)
        return remote(src.at[pl.ds(0, 4)], dst.at[pl.ds(4, 4)], hsend.at[kind, 0],
                      hrecv.at[kind, 1], tile=tile - RING)

    def halo_start(kind, up):
        acc, src = ((acck, hks), (accv, hvs))[kind]

        @pl.when(has_up if up else has_down)
        def _():
            @pl.loop(0, 4)
            def _(i):
                if up:
                    src[i + 4] = acc[i + 13].astype(BF16)
                else:
                    src[i] = acc[i + 1].astype(BF16)
            halo(kind, up).start()

    def home(kind, later):
        acc, got, out = ((acck, hk, dkb), (accv, hv, dvb))[kind]
        given = has_up if later else has_down

        @pl.when(given)
        def _():
            halo(kind, not later).wait_recv()

        @pl.loop(0, 4)
        def _(s):
            at = (z + s) % 4 + (4 if later else 0)

            @pl.when(given)
            def _():
                out[at] = (acc[at + 5] + got[at].astype(F32)).astype(BF16)

            @pl.when(jnp.logical_not(given))
            def _():
                out[at] = acc[at + 5].astype(BF16)

            back_start(2 + kind, at)

    def blk(i, size):
        return pl.ds(pl.multiple_of(i % 4 * size, size), size)

    class Line:
        def __init__(self, src, first, size, land, stage, slot):
            a, b = pl.ds(first, QUARTER), pl.ds(first + QUARTER, QUARTER)
            self.src, self.cols, self.size, self.land, self.stage = src, (a, b), size, land, stage

            def leg(i, col, n, to):
                return remote(src.at[blk(i, size), col], land.at[n], xsend.at[slot + n],
                              xrecv.at[slot + n], tile=to)

            self.rel = (leg(x + 2, a, 0, left), leg(x + 2, b, 1, right))
            self.one = (leg(x + 1, a, 2, right), leg(x + 3, b, 3, left))
            self.sum = tuple(
                remote(stage.at[n], land.at[4 + n], xsend.at[slot + 4 + n], xrecv.at[slot + 4 + n],
                       tile=(left, right)[n])
                for n in range(2)
            )

        def start(self):
            for c in self.rel + self.one:
                c.start()

        def relay(self):
            for n in range(2):
                self.rel[n].wait_recv()
                mine_too = self.src[blk(x + (3, 1)[n], self.size), self.cols[n]]
                self.stage[n] = (self.land[n].astype(F32) + mine_too.astype(F32)).astype(BF16)
                self.sum[n].start()

        def total(self, n):
            self.one[n].wait_recv()
            self.sum[n].wait_recv()
            here = self.src[blk(x, self.size), self.cols[n]]
            return here.astype(F32) + self.land[2 + n].astype(F32) + self.land[4 + n].astype(F32)

        def sent(self):
            for c in self.rel + self.one + self.sum:
                c.wait_send()

    first = Line(dwp, 0, XROWS, x1, xs1, 0)
    second = Line(y2, 0, SROWS, x2, xs2, 6)

    def half_rows(i):
        return pl.ds(pl.multiple_of(i * YROWS, YROWS), YROWS)

    y2_send = remote(dwp.at[half_rows(1 - y), pl.ds(HALF, HALF)], y2l, ysend.at[0], yrecv.at[0],
                     tile=y_pair)
    y1_send = remote(y1s, y1l, ysend.at[1], yrecv.at[1], tile=y_pair)
    to_core = remote(pos, pol, gsend.at[0], grecv.at[0], grp=other_core)
    to_y = remote(ybs, ybl, gsend.at[1], grecv.at[1], grp=other_y)

    def projected(b):
        cols = pl.ds(pl.multiple_of(b * DBLK, DBLK), DBLK)
        return jnp.dot(att_s[...], w[:, cols], preferred_element_type=F32)

    def stage_1():
        back_arrived(0)

        def part(first_head, count, blocks):
            @pl.loop(first_head, first_head + count)
            def _(h):
                rows = head_cols(h)
                turned = att_s[:, rows].T
                for b in blocks:
                    dwp[rows, b * DBLK:(b + 1) * DBLK] = jnp.dot(
                        turned, cot_s[b], preferred_element_type=F32
                    ).astype(BF16)

        per_half = HEADS // 2
        part((1 - y) * per_half, per_half, (2, 3))
        y2_send.start()
        part(0, HEADS, (0, 1))
        first.start()
        part(y * per_half, per_half, (2, 3))

        @pl.loop(0, 2)
        def _(yy):
            pos[yy] = projected(yy * 2 + 1 - core)

        to_core.start()

        @pl.loop(0, 2)
        def _(yy):
            own[yy] = projected(yy * 2 + core)

    def stage_2():
        first.relay()

    def stage_3():
        y2_send.wait_recv()
        y2[...] = (
            dwp[half_rows(y), HALF:].astype(F32) + y2l[...].astype(F32)
        ).astype(BF16)
        second.start()
        to_core.wait_recv()
        ybs[...] = (own[1 - y_hi] + pol[1 - y_hi]).astype(BF16)
        to_y.start()

    def mid_rows(i):
        return pl.ds(pl.multiple_of(i * SROWS, SROWS), SROWS)

    def stage_4():
        for n in range(2):
            cols = slice(n * QUARTER, (n + 1) * QUARTER)
            total = first.total(n)
            x_tot[n] = total
            y1s[:, cols] = x_tot[n, mid_rows(1 - y), :].astype(BF16)
        y1_send.start()
        second.relay()

    def stage_5():
        for n in range(2):
            zs[:, HALF + n * QUARTER:HALF + (n + 1) * QUARTER] = second.total(n).astype(BF16)
        y1_send.wait_recv()
        for n in range(2):
            cols = slice(n * QUARTER, (n + 1) * QUARTER)
            zs[:, cols] = (x_tot[n, mid_rows(y), :] + y1l[:, cols].astype(F32)).astype(BF16)

        @pl.loop(1, RING)
        def _(s):
            z_sum(s).start()

    def zpart(at):
        return (
            pl.ds(pl.multiple_of(at // 4 * ZROWS, ZROWS), ZROWS),
            pl.ds(pl.multiple_of(at % 4 * ZCOLS, ZCOLS), ZCOLS),
        )

    def z_sum(s):
        at = (z + s) % RING
        return remote(zs.at[zpart(at)], zl.at[z], zsend.at[0, s], zrecv.at[0, z], tile=base + at)

    def finished(at):
        row = jnp.where(at % 4 < 2, x * XROWS + y * SROWS, y * YROWS + x * SROWS)
        rows = pl.ds(pl.multiple_of(row + at // 4 * ZROWS, ZROWS), ZROWS)
        return dw.at[rows, zpart(at)[1]]

    def z_all(s):
        at = (z + s) % RING
        return remote(fin, finished(z), zsend.at[1, s], zrecv.at[1, z], tile=base + at)

    fin_own = pltpu.make_async_copy(fin, finished(z), olocal.at[4])

    def stage_6():
        rows, cols = zpart(z)
        total = zs[rows, cols].astype(F32)
        for s in range(1, RING):
            at = (z + s) % RING
            remote(zl.at[at], zl.at[at], zsend.at[0, 0], zrecv.at[0, at], tile=base + at).wait_recv()
            total += zl[at].astype(F32)
        fin[...] = total.astype(BF16)

        @pl.loop(1, RING)
        def _(s):
            z_all(s).start()

        fin_own.start()

    lo, hi = pl.ds(0, HALF), pl.ds(HALF, HALF)

    def slab_1y(yy):
        return dw.at[pl.ds(pl.multiple_of(x * XROWS + yy * SROWS, SROWS), SROWS), lo]

    def slab_2y(yy):
        return dw.at[half_rows(yy), hi]

    all_1y = remote(slab_1y(y), slab_1y(y), ysend.at[2], yrecv.at[2], tile=y_pair)
    got_1y = remote(slab_1y(1 - y), slab_1y(1 - y), ysend.at[2], yrecv.at[2], tile=y_pair)
    all_2y = remote(slab_2y(y), slab_2y(y), ysend.at[3], yrecv.at[3], tile=y_pair)
    got_2y = remote(slab_2y(1 - y), slab_2y(1 - y), ysend.at[3], yrecv.at[3], tile=y_pair)

    class Spread:
        def __init__(self, rows, cols, slot):
            def part(i, n, k, to):
                ref = dw.at[rows(i), pl.ds(cols + n * QUARTER, QUARTER)]
                return remote(ref, ref, xsend.at[slot + k], xrecv.at[slot + k], tile=to)

            self.outs = (
                part(x, 0, 0, right), part(x, 1, 1, left), part(x, 1, 2, right), part(x, 0, 3, left)
            )
            self.near = (part(x + 3, 0, 0, left), part(x + 1, 1, 1, right))
            self.on = (part(x + 3, 0, 4, right), part(x + 1, 1, 5, left))
            self.rest = (
                part(x + 3, 1, 2, left), part(x + 1, 0, 3, right),
                part(x + 2, 0, 4, left), part(x + 2, 1, 5, right),
            )

        def start(self):
            for c in self.outs:
                c.start()

        def relay(self):
            for n in range(2):
                self.near[n].wait_recv()
                self.on[n].start()

        def finish(self):
            for c in self.rest:
                c.wait_recv()

        def sent(self):
            for c in self.outs + self.on:
                c.wait_send()

    spread_1 = Spread(lambda i: blk(i, XROWS), 0, 12)
    spread_2 = Spread(
        lambda i: pl.ds(pl.multiple_of(y * YROWS + i % 4 * SROWS, SROWS), SROWS), HALF, 18
    )

    def stage_7():
        @pl.loop(1, RING)
        def _(s):
            at = (z + s) % RING
            remote(fin, finished(at), zsend.at[1, 0], zrecv.at[1, at], tile=base + at).wait_recv()

        fin_own.wait()
        spread_2.start()
        all_1y.start()

    def stage_8():
        spread_2.relay()
        got_1y.wait_recv()
        spread_1.start()
        to_y.wait_recv()
        bo[...] = (own[y_hi] + pol[y_hi] + ybl[...].astype(F32)).astype(BF16)

    def stage_9():
        spread_2.finish()
        all_2y.start()
        spread_1.relay()

    def stage_10():
        got_2y.wait_recv()
        spread_1.finish()

    @pl.when(mine)
    def _():
        acck[...] = jnp.zeros_like(acck)
        accv[...] = jnp.zeros_like(accv)
        tmp[NB] = jnp.zeros((TILE, HEAD_DIM), F32)
        keep(0).wait()
        hop(0, z, True)

        @pl.loop(1, RING)
        def _(s):
            at = (z + RING - s) % RING
            arrived(0, at).wait_recv()
            hop(0, at, True)

        keep(4).wait()

        @pl.loop(1, RING)
        def _(s):
            arrived(4, (z + RING - s) % RING).wait_recv()

        lists = pltpu.make_async_copy(nb_v, nb_s, lsem.at[5])
        lists.start()
        hops_arrived(0)
        lists.wait()

        def ready(kind, i):
            @pl.when(i == 0)
            def _():
                keep(kind).wait()

            @pl.when(i > 0)
            def _():
                arrived(kind, (z + RING - i) % RING).wait_recv()

        @pl.loop(0, RING)
        def _(i):
            ready(2, i)
            weigh((z + RING - i) % RING)

            @pl.when(i >= 4)
            def _():
                for n in range(2):
                    s = (i - 4) * 2 + n
                    ready(1, s)
                    hop(1, (z + RING - s) % RING, True)

        hops_arrived(1)

        @pl.loop(0, RING)
        def _(i):
            r = (z + RING - i) % RING
            attend(r)
            back_start(0, r)

    @pl.when(jnp.logical_not(mine))
    def _():
        @pl.loop(1, RING)
        def _(s):
            at = (z + s) % RING

            @pl.when(owns(at, idle))
            def _():
                send(1, at).wait_send()

    send_kinds((3,))
    stage_1()

    def steps(work, stages):
        @pl.loop(0, RING)
        def _(i):
            pl.when(mine)(lambda: work(i))
            for n, stage in stages:
                pl.when(i == n)(stage)

    def owner(stage):
        def run():
            @pl.when(mine)
            def _():
                stage()

        return run

    def value_step(i):
        @pl.when(i == 0)
        def _():
            keep(3).wait()

        @pl.when(i > 0)
        def _():
            arrived(3, (z + RING - i) % RING).wait_recv()

        value_part((z + RING - i) % RING)

    def query_step(i):
        r = (z + i) % RING
        query_part(r)
        back_start(1, r)

    steps(value_step, ((5, stage_2), (7, owner(lambda: (halo_start(1, False), halo_start(1, True))))))
    steps(
        key_part,
        (
            (1, stage_3), (3, stage_4), (4, stage_5), (4, owner(lambda: (home(1, True), home(1, False)))),
            (4, owner(lambda: halo_start(0, False))), (6, stage_6),
            (7, owner(lambda: halo_start(0, True))), (7, owner(lambda: home(0, True))),
        ),
    )
    steps(
        query_step,
        ((1, stage_7), (2, owner(lambda: home(0, False))), (3, stage_8), (6, stage_9)),
    )
    stage_10()

    for kind in (1, 2, 3):
        back_arrived(kind)

    @pl.loop(1, RING)
    def _(s):
        at = (z + s) % RING

        @pl.when(owns(at, idle))
        def _():
            for kind in (0, 2, 3, 4):
                send(kind, at).wait_send()

            @pl.when(mine)
            def _():
                send(1, at).wait_send()

        @pl.when(mine)
        def _():
            for kind in range(4):
                back(kind, at).wait_send()

        z_sum(s).wait_send()
        z_all(s).wait_send()

    @pl.when(mine)
    def _():
        @pl.loop(0, RING)
        def _(at):
            for kind in (0, 1):
                hop(kind, at, False)

        for kind in (0, 1):
            @pl.when(has_down)
            def _():
                halo(kind, False).wait_send()

            @pl.when(has_up)
            def _():
                halo(kind, True).wait_send()

    for c in (cot_y, cot_core, cot_on, y2_send, y1_send, to_core, to_y, all_1y, all_2y):
        c.wait_send()
    for c in (first, second, spread_1, spread_2):
        c.sent()


def step(listed, tokens, q, k, v, cot, w):
    any_space = pl.BlockSpec(memory_space=pl.ANY)
    vmem = pl.BlockSpec(memory_space=pltpu.VMEM)
    smem = pl.BlockSpec(memory_space=pltpu.SMEM)
    dma = pltpu.SemaphoreType.DMA
    grad = jax.ShapeDtypeStruct((TILE, FEAT), BF16)

    def tiles(n, dtype=BF16):
        return pltpu.VMEM((n, TILE, HEAD_DIM), dtype)

    return pl.pallas_call(
        step_kernel,
        out_shape=(
            jax.ShapeDtypeStruct((TILE, DBLK), BF16), grad, grad, grad,
            jax.ShapeDtypeStruct((FEAT, DOUT), BF16),
        ),
        in_specs=[smem, smem, any_space, any_space, any_space, vmem, vmem],
        out_specs=(vmem, any_space, any_space, any_space, any_space),
        scratch_shapes=[
            pltpu.VMEM((8, 128), jnp.int32),
            pltpu.VMEM((RING, 8, 128), jnp.int32),
            pltpu.SMEM((RING, 8, 128), jnp.int32),
            tiles(2 * RING),
            tiles(2 * RING),
            tiles(RING),
            tiles(RING),
            pltpu.VMEM((GRP, TILE, DBLK), BF16),
            tiles(HEADS),
            pltpu.VMEM((KEYS, TILE), F32),
            pltpu.VMEM((RING, KEYS, TILE), BF16),
            pltpu.VMEM((KEYS, HEAD_DIM), BF16),
            tiles(NB + 1, F32),
            pltpu.VMEM((RING, HEAD_DIM, TILE), F32),
            tiles(2 * RING + 2, F32),
            tiles(2 * RING + 2, F32),
            tiles(RING),
            tiles(RING),
            pltpu.VMEM((TILE, FEAT), BF16),
            tiles(RING),
            tiles(RING),
            tiles(RING),
            tiles(RING),
            tiles(RING),
            tiles(RING),
            pltpu.VMEM((FEAT, DOUT), BF16),
            pltpu.VMEM((6, XROWS, QUARTER), BF16),
            pltpu.VMEM((6, SROWS, QUARTER), BF16),
            pltpu.VMEM((2, XROWS, QUARTER), BF16),
            pltpu.VMEM((2, SROWS, QUARTER), BF16),
            pltpu.VMEM((2, XROWS, QUARTER), F32),
            pltpu.VMEM((SROWS, HALF), BF16),
            pltpu.VMEM((SROWS, HALF), BF16),
            pltpu.VMEM((YROWS, HALF), BF16),
            pltpu.VMEM((YROWS, HALF), BF16),
            pltpu.VMEM((SROWS, DOUT), BF16),
            pltpu.VMEM((RING, ZROWS, ZCOLS), BF16),
            pltpu.VMEM((ZROWS, ZCOLS), BF16),
            pltpu.VMEM((2, TILE, DBLK), F32),
            pltpu.VMEM((2, TILE, DBLK), F32),
            pltpu.VMEM((2, TILE, DBLK), F32),
            pltpu.VMEM((TILE, DBLK), BF16),
            pltpu.VMEM((TILE, DBLK), BF16),
            dma((5, RING)),
            dma((5, RING)),
            dma((6,)),
            dma((3,)),
            dma((3,)),
            dma((1,)),
            dma((2, RING)),
            dma((2, RING)),
            dma((4, RING)),
            dma((4, HEADS)),
            dma((5,)),
            dma((2, 2)),
            dma((2, 2)),
            dma((24,)),
            dma((24,)),
            dma((4,)),
            dma((4,)),
            dma((2, RING)),
            dma((2, RING)),
            dma((2,)),
            dma((2,)),
        ],
        compiler_params=pltpu.CompilerParams(
            collective_id=0, has_side_effects=True, vmem_limit_bytes=VMEM_LIMIT
        ),
        name="step",
    )(listed, tokens, q, k, v, cot, w)


def settle_kernel(*refs):
    count = (len(refs) - 1) // 3
    sems = refs[-1]

    def moves(n, part, leg):
        src, dst, held = refs[n], refs[count + n], refs[2 * count + n]
        rows = src.shape[0] // 4
        here = pl.ds(part * rows, rows)
        if leg == 0:
            return pltpu.make_async_copy(src.at[here], held.at[here], sems.at[0, n, part])
        return pltpu.make_async_copy(held.at[here], dst.at[here], sems.at[1, n, part])

    every = [(n, part) for n in range(count) for part in range(4)]
    for n, part in every:
        moves(n, part, 0).start()
    for n, part in every:
        moves(n, part, 0).wait()
        moves(n, part, 1).start()
    for n, part in every:
        moves(n, part, 1).wait()


def settle(arrays):
    any_space = pl.BlockSpec(memory_space=pl.ANY)
    return pl.pallas_call(
        settle_kernel,
        out_shape=tuple(jax.ShapeDtypeStruct(a.shape, a.dtype) for a in arrays),
        in_specs=[any_space] * len(arrays),
        out_specs=(any_space,) * len(arrays),
        scratch_shapes=[pltpu.VMEM(a.shape, a.dtype) for a in arrays]
        + [pltpu.SemaphoreType.DMA((2, len(arrays), 4))],
        compiler_params=pltpu.CompilerParams(vmem_limit_bytes=VMEM_LIMIT),
        name="settle",
    )(*arrays)


def body(query_tokens, key_tokens, value_tokens, w_out, cotangent, neighbours, tile_tokens):
    return settle(
        step(neighbours, tile_tokens, query_tokens, key_tokens, value_tokens, cotangent, w_out)
    )


def solution(mesh):
    placed = (
        P("tile", "grp"),
        P("tile", "grp"),
        P("tile", "grp"),
        P("grp", None),
        P("tile", "grp"),
        P("tile", None),
        P(),
    )
    return jax.shard_map(
        body,
        mesh=mesh,
        in_specs=placed,
        out_specs=(
            P("tile", "grp"),
            P("tile", "grp"),
            P("tile", "grp"),
            P("tile", "grp"),
            P("grp", None),
        ),
        check_vma=False,
    )
```
